32 devices in a mesh: section: 4 (over z), ctx: 8 (over y, x, core).
Axes of the slice: x: 2, y: 2, z: 4, core: 2. Of those that a mesh axis runs over, the one named last changes fastest.
Arguments:
- queries: bfloat16 [8, 1280, 3072], P('section', 'ctx'), may hold values from -28 to 28, as said below
- cotangent: bfloat16 [8, 1280, 3072], P('section', 'ctx'), may hold values from -6 to 6
- ret_query: bfloat16 [1280, 3072], P('ctx', 'section'), may hold values from -6 to 6
- ret_key: bfloat16 [1280, 3072], P('ctx', 'section'), may hold values from -6 to 6
- ret_value: bfloat16 [1280, 3072], P('ctx', 'section'), may hold values from -6 to 6
- gate_log: float32 [1280, 24], P('ctx', 'section'), may hold values from -1.5 to 0, as said below
- kv_weight: bfloat16 [3072, 2048], P('section'), may hold values from -0.109375 to 0.109375
Outputs:
- attention: bfloat16 [8, 1280, 3072], P('section', 'ctx')
- query_grad: bfloat16 [8, 1280, 3072], P('section', 'ctx')
- retention_grad: bfloat16 [1280, 3072], P('ctx', 'section')
The draws below stay inside these ranges and needn't reach their ends.
Inputs may be any that keep to these rules, and one draw needn't show every extreme that they name: The attention queries are mostly of order one; a few rows may be scaled by up to 16. `gate_log`: every gate is below one.
All inputs are finite; a program needn't handle non-finite values.
Results may differ from the reference program's by a relative error of at most 0.034.
Values may be sent and summed in bfloat16 or wider, within the bound.
A program may use at most 640 MiB of HBM per device.

```python
import math
import jax
import jax.numpy as jnp
from jax import lax

HEADS = 24
DH = 128
KV_HEADS = 8
D = 3072
N_LAYERS = 8
TOK_DEV = 160
TOKENS = 1280


def draw_queries(key, part):
    key = jax.random.fold_in(key, 11)
    first_key = jax.random.fold_in(key, 0)
    shape = (N_LAYERS, TOKENS, D)
    drawn = jnp.clip(jax.random.normal(first_key, shape, jnp.float32), -4.0, 4.0)
    return drawn.astype(jnp.bfloat16)


def draw_gate_log(key, part):
    key = jax.random.fold_in(key, 23)
    keys_list = jax.random.split(key, 6)
    fast_share = 0.5
    fast = jax.random.uniform(keys_list[0], (HEADS,), jnp.float32) < fast_share
    slow_rate = jnp.exp(jax.random.uniform(keys_list[1], (HEADS,), jnp.float32, math.log(0.1), math.log(0.9))) * (math.log(2.5) / TOKENS)
    fast_rate = jnp.exp(jax.random.uniform(keys_list[2], (HEADS,), jnp.float32, math.log(1.0 / 50.0), math.log(1.0 / 30.0)))
    per_channel_fading = jnp.where(fast, fast_rate, slow_rate)
    sampled_perturbation = jax.random.uniform(keys_list[3], (TOKENS, HEADS), jnp.float32, 0.5, 1.5)
    spots = jax.random.randint(keys_list[4], (2, HEADS), 0, TOKENS)
    objective_scores = jax.random.uniform(keys_list[5], (2, HEADS), jnp.float32, math.log(0.5), math.log(0.8))
    placed_sequence = jnp.arange(TOKENS, dtype=jnp.int32)[:, None, None] == spots[None]
    token_batches = jnp.sum(jnp.where(placed_sequence, objective_scores[None], 0.0), axis=1)
    return (token_batches - per_channel_fading[None, :] * sampled_perturbation).astype(jnp.float32)


def block_levels(stream_key, shape, cuts, least, high):
    def one(position, shards_of):
        steps = jax.random.uniform(jax.random.fold_in(jax.random.fold_in(stream_key, 6), position), (shards_of,), jnp.float32, least / len(cuts), high / len(cuts))
        return jnp.repeat(jnp.exp(steps), shape[position] // shards_of).reshape((-1,) + (1,) * (len(shape) - position - 1))

    factor_of = one(*cuts[0])
    for cut in cuts[1:]:
        factor_of = factor_of * one(*cut)
    return factor_of


def normal_values(key, extent, deviation, limit, pieces=(), kind=jnp.bfloat16):
    entries = deviation * jax.random.normal(key, extent, jnp.float32)
    if pieces:
        entries = entries * block_levels(key, extent, pieces, -0.22, 0.18)
    return jnp.clip(entries, -limit, limit).astype(kind)


def setup_inputs(seed: int = 0) -> dict:
    arg_keys = jax.random.split(jax.random.key(seed), 8)
    queries = draw_queries(jax.random.fold_in(arg_keys[7], 71), 0)
    cotangent = normal_values(arg_keys[1], (N_LAYERS, TOKENS, D), 1.0, 6.0, ((0, 4), (1, 8)))
    ret_query = normal_values(arg_keys[2], (TOKENS, D), 1.0, 6.0, ((0, 8), (1, 4)))
    ret_key = normal_values(arg_keys[3], (TOKENS, D), 1.0, 6.0, ((0, 8), (1, 4)))
    ret_value = normal_values(arg_keys[4], (TOKENS, D), 1.0, 6.0, ((0, 8), (1, 4)))
    gate_log = draw_gate_log(jax.random.fold_in(arg_keys[7], 71), 0)
    kv_weight = normal_values(arg_keys[6], (D, 2 * KV_HEADS * DH), D ** -0.5, 0.109375, ((0, 4),))
    return {"queries": queries, "cotangent": cotangent, "ret_query": ret_query, "ret_key": ret_key, "ret_value": ret_value, "gate_log": gate_log, "kv_weight": kv_weight}


epsilon = 1e-06
highest = lax.Precision.HIGHEST

def retention_block(state_before, inputs):
    query_part, key_part, value_part, gate_part = inputs
    cumulative = jnp.cumsum(gate_part, axis=0)
    places = jnp.arange(gate_part.shape[0], dtype=jnp.int32)
    causal = places[:, None] >= places[None, :]
    spread = cumulative.T[:, :, None] - cumulative.T[:, None, :]
    weights = jnp.exp(jnp.where(causal[None], spread, -jnp.inf))
    scores = jnp.einsum('thd,uhd->htu', query_part, key_part, precision=highest)
    inside = jnp.einsum('htu,uhd->thd', weights * scores, value_part, precision=highest)
    carried = jnp.einsum('thd,hde->the', query_part, state_before, precision=highest)
    raw_output = inside + jnp.exp(cumulative)[:, :, None] * carried
    tail_decay = jnp.exp(cumulative[-1][None, :] - cumulative)
    local_state = jnp.einsum('uh,uhd,uhe->hde', tail_decay, key_part, value_part, precision=highest)
    state_after = jnp.exp(cumulative[-1])[:, None, None] * state_before + local_state
    return (state_after, raw_output)

def reference(queries, cotangent, ret_query, ret_key, ret_value, gate_log, kv_weight):
    block_total = TOKENS // TOK_DEV

    def to_blocks(array):
        return array.astype(jnp.float32).reshape(block_total, TOK_DEV, HEADS, DH)
    gate_blocks = gate_log.reshape(block_total, TOK_DEV, HEADS)
    start_state = jnp.zeros((HEADS, DH, DH), jnp.float32)
    _, raw_output = lax.scan(retention_block, start_state, (to_blocks(ret_query), to_blocks(ret_key), to_blocks(ret_value), gate_blocks))
    raw_output = raw_output.reshape(TOKENS, HEADS, DH)
    normed = raw_output * lax.rsqrt(lax.optimization_barrier(jnp.mean(raw_output * raw_output, axis=-1, keepdims=True)) + epsilon)
    ret_out = normed.astype(jnp.bfloat16).reshape(TOKENS, D)
    cache = jnp.dot(ret_out, kv_weight, preferred_element_type=jnp.float32).astype(jnp.bfloat16)
    kv_width = KV_HEADS * DH
    cache_wide = lax.optimization_barrier(cache).astype(jnp.float32)
    cache_keys = cache_wide[:, :kv_width].reshape(TOKENS, KV_HEADS, DH)
    cache_values = cache_wide[:, kv_width:].reshape(TOKENS, KV_HEADS, DH)
    group_size = HEADS // KV_HEADS
    score_scale = 1.0 / math.sqrt(DH)
    block_rows = math.gcd(512, TOKENS)

    def one_layer(cache_term, layer_inputs):
        query_layer, grad_layer = layer_inputs
        attended_list = []
        grad_list = []
        for first_row in range(0, TOKENS, block_rows):
            last_row = first_row + block_rows
            query_block = query_layer[first_row:last_row].astype(jnp.float32).reshape(block_rows, KV_HEADS, group_size, DH)
            grad_block = grad_layer[first_row:last_row].astype(jnp.float32).reshape(block_rows, KV_HEADS, group_size, DH)
            key_block = cache_keys[:last_row]
            value_block = cache_values[:last_row]
            scores = jnp.einsum('rkgd,ukd->kgru', query_block, key_block, precision=highest) * score_scale
            visible = (first_row + jnp.arange(block_rows, dtype=jnp.int32))[:, None] >= jnp.arange(last_row, dtype=jnp.int32)[None, :]
            scores = jnp.where(visible, scores, -jnp.inf)
            row_top = lax.optimization_barrier(jnp.max(scores, axis=-1, keepdims=True))
            row_total = lax.optimization_barrier(jnp.sum(jnp.exp(scores - row_top), axis=-1, keepdims=True))
            soft_probs = jnp.exp(scores - row_top) / row_total
            probs_low = lax.optimization_barrier(soft_probs.astype(jnp.bfloat16)).astype(jnp.float32)
            mixed_output = jnp.einsum('kgru,ukd->rkgd', probs_low, value_block, precision=highest).astype(jnp.bfloat16)
            attended_wide = lax.optimization_barrier(mixed_output).astype(jnp.float32)
            row_delta = jnp.einsum('rkgd,rkgd->kgr', grad_block, attended_wide, precision=highest)
            prob_grad = jnp.einsum('rkgd,ukd->kgru', grad_block, value_block, precision=highest)
            score_grad = (soft_probs * (prob_grad - row_delta[..., None]) * score_scale).astype(jnp.bfloat16)
            score_wide = lax.optimization_barrier(score_grad).astype(jnp.float32)
            query_part = jnp.einsum('kgru,ukd->rkgd', score_wide, key_block, precision=highest).astype(jnp.bfloat16)
            key_grad = jnp.einsum('kgru,rkgd->ukd', score_wide, query_block, precision=highest)
            value_grad = jnp.einsum('kgru,rkgd->ukd', probs_low, grad_block, precision=highest)
            rows_term = jnp.concatenate([key_grad.reshape(last_row, kv_width), value_grad.reshape(last_row, kv_width)], axis=1)
            cache_term = cache_term.at[:last_row].add(rows_term)
            attended_list.append(mixed_output.reshape(block_rows, D))
            grad_list.append(query_part.reshape(block_rows, D))
        return (cache_term, (jnp.concatenate(attended_list, axis=0), jnp.concatenate(grad_list, axis=0)))
    start_term = jnp.zeros((TOKENS, 2 * kv_width), jnp.float32)
    cache_term, outputs = lax.scan(one_layer, start_term, (queries, cotangent))
    attention, query_grad = outputs
    cache_grad = cache_term.astype(jnp.bfloat16)
    retention_grad = jnp.dot(cache_grad, kv_weight.T, preferred_element_type=jnp.float32).astype(jnp.bfloat16)
    return (attention, query_grad, retention_grad)
```

```python
import math

import jax
import jax.numpy as jnp
from jax import lax
from jax.experimental import pallas as pl
from jax.experimental.pallas import tpu as pltpu
from jax.sharding import PartitionSpec as P

DH = 128


epsilon = 1e-06
highest = lax.Precision.HIGHEST


def entering(value, axis, join, neutral):
    count, mine = (lax.axis_size(axis), lax.axis_index(axis))
    pieces = jax.tree.map(lambda part: lax.all_gather(part, axis), value)
    running = jax.tree.map(
        lambda part, zero: jnp.full_like(part, 0) + jnp.asarray(zero, part.dtype), value, neutral
    )

    def lap(position, running):
        longer = join(running, jax.tree.map(lambda part: part[position], pieces))
        return jax.tree.map(lambda new, old: jnp.where(position < mine, new, old), longer, running)

    return lax.fori_loop(0, count - 1, lap, running)


def combine_state(earlier, later):
    return (earlier[0] * later[0], later[0][:, None, None] * earlier[1] + later[1])


def kept_memory_lines(ret_query, ret_key, ret_value, gate_log):
    row_count, heads_here = gate_log.shape
    head_width = ret_query.shape[1] // heads_here
    query_part = ret_query.astype(jnp.float32).reshape(row_count, heads_here, head_width)
    key_part = ret_key.astype(jnp.float32).reshape(row_count, heads_here, head_width)
    value_part = ret_value.astype(jnp.float32).reshape(row_count, heads_here, head_width)
    cumulative = jnp.cumsum(gate_log, axis=0)
    places = jnp.arange(row_count, dtype=jnp.int32)
    causal = places[:, None] >= places[None, :]
    spread = cumulative.T[:, :, None] - cumulative.T[:, None, :]
    weights = jnp.exp(jnp.where(causal[None], spread, -jnp.inf))
    scores = jnp.einsum("thd,uhd->htu", query_part, key_part, precision=highest)
    inside = jnp.einsum("htu,uhd->thd", weights * scores, value_part, precision=highest)
    tail_decay = jnp.exp(cumulative[-1][None, :] - cumulative)
    local_state = jnp.einsum("uh,uhd,uhe->hde", tail_decay, key_part, value_part, precision=highest)
    decay_total = jnp.exp(cumulative[-1])
    identity = (jnp.ones_like(decay_total), jnp.zeros_like(local_state))
    scanned = entering((decay_total, local_state), "ctx", combine_state, identity)
    state_before = scanned[1]
    carried = jnp.einsum("thd,hde->the", query_part, state_before, precision=highest)
    raw_output = inside + jnp.exp(cumulative)[:, :, None] * carried
    normed = raw_output * lax.rsqrt(
        jnp.mean(raw_output * raw_output, axis=-1, keepdims=True) + epsilon
    )
    return normed.astype(jnp.bfloat16).reshape(row_count, heads_here * head_width)


def attention_kernel(ctx_ref, q_ref, g_ref, k_ref, v_ref, att_ref, qg_ref, kg_ref, vg_ref):
    layer_count, row_count, width = q_ref.shape
    group = width // DH
    total = k_ref.shape[0]
    columns = group * row_count
    scale = 1.0 / math.sqrt(DH)
    keys = k_ref[...]
    values = v_ref[...]
    key_place = lax.broadcasted_iota(jnp.int32, (total, row_count), 0)
    row_place = ctx_ref[0] * row_count + lax.broadcasted_iota(jnp.int32, (total, row_count), 1)
    visible = jnp.concatenate([jnp.where(key_place <= row_place, 0.0, -jnp.inf)] * group, axis=1)

    def stacked(ref, layer):
        return jnp.concatenate(
            [ref[layer, :, j * DH : (j + 1) * DH] for j in range(group)], axis=0
        )

    def spread(ref, layer, rows):
        for j in range(group):
            ref[layer, :, j * DH : (j + 1) * DH] = rows[j * row_count : (j + 1) * row_count]

    key_grad = jnp.zeros((total, DH), jnp.float32)
    value_grad = jnp.zeros((total, DH), jnp.float32)
    for layer in range(layer_count):
        queries = stacked(q_ref, layer)
        grads = stacked(g_ref, layer)
        scores = lax.dot_general(
            keys, queries, (((1,), (1,)), ((), ())), preferred_element_type=jnp.float32
        )
        scores = scores * scale + visible
        top = jnp.max(scores, axis=0, keepdims=True)
        soft = jnp.exp(scores - top)
        soft = soft * (1.0 / jnp.sum(soft, axis=0, keepdims=True))
        low = soft.astype(jnp.bfloat16)
        mixed = lax.dot_general(
            low, values, (((0,), (0,)), ((), ())), preferred_element_type=jnp.float32
        ).astype(jnp.bfloat16)
        spread(att_ref, layer, mixed)
        product = grads.astype(jnp.float32) * mixed.astype(jnp.float32)
        delta = jnp.sum(product.T, axis=0, keepdims=True)
        prob_grad = lax.dot_general(
            values, grads, (((1,), (1,)), ((), ())), preferred_element_type=jnp.float32
        )
        score_grad = (soft * (prob_grad - delta) * scale).astype(jnp.bfloat16)
        query_grad = lax.dot_general(
            score_grad, keys, (((0,), (0,)), ((), ())), preferred_element_type=jnp.float32
        )
        spread(qg_ref, layer, query_grad.astype(jnp.bfloat16))
        key_grad += jnp.dot(score_grad, queries, preferred_element_type=jnp.float32)
        value_grad += jnp.dot(low, grads, preferred_element_type=jnp.float32)
    kg_ref[...] = key_grad.astype(kg_ref.dtype)
    vg_ref[...] = value_grad.astype(vg_ref.dtype)


def cross_attention(queries, cotangent, full_cache, place):
    layer_count, row_count, model_width = queries.shape
    total, cache_width = full_cache.shape
    kv_heads = cache_width // 2 // DH
    width = model_width // kv_heads
    rows = pl.BlockSpec((layer_count, row_count, width), lambda h, c: (0, 0, h))
    cut = pl.BlockSpec((total, DH), lambda h, c: (0, h))
    cut_values = pl.BlockSpec((total, DH), lambda h, c: (0, kv_heads + h))
    half = jax.ShapeDtypeStruct((total, cache_width // 2), jnp.float32)
    return pl.pallas_call(
        attention_kernel,
        grid_spec=pltpu.PrefetchScalarGridSpec(
            num_scalar_prefetch=1,
            grid=(kv_heads,),
            in_specs=[rows, rows, cut, cut_values],
            out_specs=[rows, rows, cut, cut],
        ),
        out_shape=[
            jax.ShapeDtypeStruct(queries.shape, jnp.bfloat16),
            jax.ShapeDtypeStruct(queries.shape, jnp.bfloat16),
            half,
            half,
        ],
        compiler_params=pltpu.CompilerParams(vmem_limit_bytes=56 * 1024 * 1024),
    )(place, queries, cotangent, full_cache, full_cache)


def body(queries, cotangent, ret_query, ret_key, ret_value, gate_log, kv_weight):
    ret_out = kept_memory_lines(ret_query, ret_key, ret_value, gate_log)
    partial_rows = jnp.dot(ret_out, kv_weight, preferred_element_type=jnp.float32)
    cache = lax.psum(partial_rows, "section").astype(jnp.bfloat16)
    full_cache = lax.all_gather(cache, "ctx", axis=0, tiled=True)
    place = lax.axis_index("ctx").reshape(1)
    attended_all, grad_rows_all, key_grad, value_grad = cross_attention(
        queries, cotangent, full_cache, place
    )
    cache_total = jnp.concatenate([key_grad, value_grad], axis=1)
    own_part = lax.psum_scatter(cache_total, "ctx", scatter_dimension=0, tiled=True)
    summed_grad = lax.psum(own_part, "section")
    cache_grad = summed_grad.astype(jnp.bfloat16)
    retention_grad = jnp.einsum(
        "rw,cw->rc", cache_grad, kv_weight, preferred_element_type=jnp.float32
    ).astype(jnp.bfloat16)
    return (attended_all, grad_rows_all, retention_grad)


def solution(mesh):
    return jax.shard_map(
        body,
        mesh=mesh,
        in_specs=(
            P("section", "ctx", None),
            P("section", "ctx", None),
            P("ctx", "section"),
            P("ctx", "section"),
            P("ctx", "section"),
            P("ctx", "section"),
            P("section", None),
        ),
        out_specs=(P("section", "ctx", None), P("section", "ctx", None), P("ctx", "section")),
        check_vma=False,
    )
```

```python
import functools
import math

import jax
import jax.numpy as jnp
from jax import lax
from jax.experimental import pallas as pl
from jax.experimental.pallas import tpu as pltpu
from jax.sharding import PartitionSpec as P

DH = 128


epsilon = 1e-06
highest = lax.Precision.HIGHEST

MESH = pl.DeviceIdType.MESH
LIMIT = 56 * 1024 * 1024


def greet(peers):
    barrier = pltpu.get_barrier_semaphore()
    for peer in peers:
        pl.semaphore_signal(barrier, inc=1, device_id=peer, device_id_type=MESH)
    pl.semaphore_wait(barrier, len(peers))


def remote(source, target, send_sem, recv_sem, device):
    return pltpu.make_async_remote_copy(
        src_ref=source,
        dst_ref=target,
        send_sem=send_sem,
        recv_sem=recv_sem,
        device_id=device,
        device_id_type=MESH,
    )


def two_part_dot(wide, narrow, dims):
    high = wide.astype(jnp.bfloat16)
    low = (wide - high.astype(jnp.float32)).astype(jnp.bfloat16)
    return lax.dot_general(
        high, narrow, dims, preferred_element_type=jnp.float32
    ) + lax.dot_general(low, narrow, dims, preferred_element_type=jnp.float32)


def cache_kernel(
    n_sec,
    n_ctx,
    q_ref,
    k_ref,
    v_ref,
    gate_ref,
    turned_ref,
    w_ref,
    out_ref,
    ret,
    raw,
    own_state,
    own_total,
    sib_state,
    sib_total,
    chip_state,
    chip_total,
    got_state,
    got_total,
    running,
    send_part,
    got_part,
    sib_send,
    sib_recv,
    st_send,
    st_recv,
    tot_send,
    tot_recv,
    part_send,
    part_recv,
    z_send,
    z_recv,
    x_send,
    x_recv,
    y_send,
    y_recv,
):
    sec, ctx = lax.axis_index("section"), lax.axis_index("ctx")
    chip, core = lax.div(ctx, 2), lax.rem(ctx, 2)
    n_chip = n_ctx // 2
    sibling = (sec, chip * 2 + 1 - core)
    rows, width = q_ref.shape
    heads = width // DH
    columns = out_ref.shape[1]
    piece = columns // n_sec
    half = columns // 2
    row_dims = (((0,), (0,)), ((), ()))
    plain = (((1,), (0,)), ((), ()))
    last_dims = (((1,), (1,)), ((), ()))

    greet(
        [(lax.rem(sec + j, n_sec), ctx) for j in range(1, n_sec)]
        + [(sec, lax.rem(ctx + j, n_ctx)) for j in range(1, n_ctx)]
    )

    first = lax.broadcasted_iota(jnp.int32, (rows, rows), 0)
    second = lax.broadcasted_iota(jnp.int32, (rows, rows), 1)
    causal = first >= second
    cumulative = jnp.dot(
        causal.astype(jnp.float32), gate_ref[...], precision=highest,
        preferred_element_type=jnp.float32,
    )
    turned = jnp.dot(
        turned_ref[...], (first <= second).astype(jnp.float32), precision=highest,
        preferred_element_type=jnp.float32,
    )
    total = cumulative[rows - 1 : rows]
    own_total[...] = jnp.broadcast_to(total, own_total.shape)
    tail = jnp.exp(total - cumulative)
    for h in range(heads):
        cut = slice(h * DH, (h + 1) * DH)
        decayed = k_ref[:, cut].astype(jnp.float32) * tail[:, h : h + 1]
        own_state[h] = two_part_dot(decayed, v_ref[:, cut], row_dims).astype(jnp.bfloat16)

    def to_sibling(index):
        pair = ((own_state, sib_state), (own_total, sib_total))[index]
        return remote(*pair, sib_send.at[index], sib_recv.at[index], sibling)

    @pl.when(core == 0)
    def _():
        to_sibling(0).start()
        to_sibling(1).start()

    def chip_copy(r, c, index):
        if index == 0:
            return remote(
                chip_state, got_state.at[chip], st_send.at[r, c], st_recv.at[chip], (sec, 2 * r + c)
            )
        return remote(
            chip_total, got_total.at[chip], tot_send.at[r, c], tot_recv.at[chip], (sec, 2 * r + c)
        )

    @pl.when(core == 1)
    def _():
        to_sibling(0).wait_recv()
        to_sibling(1).wait_recv()
        chip_total[...] = own_total[...] + sib_total[...]
        kept = jnp.exp(total)
        for h in range(heads):
            chip_state[h] = (
                sib_state[h].astype(jnp.float32) * kept[:, h : h + 1]
                + own_state[h].astype(jnp.float32)
            ).astype(jnp.bfloat16)
        for r in range(n_chip - 1, 0, -1):

            @pl.when(chip < r)
            def _():
                for c in range(2):
                    chip_copy(r, c, 1).start()
                    chip_copy(r, c, 0).start()

    for h in range(heads):
        cut = slice(h * DH, (h + 1) * DH)
        spread = cumulative[:, h : h + 1] - turned[h : h + 1, :]
        weights = jnp.exp(jnp.where(causal, spread, -jnp.inf))
        scores = lax.dot_general(
            q_ref[:, cut], k_ref[:, cut], last_dims, preferred_element_type=jnp.float32
        )
        raw[:, cut] = two_part_dot(weights * scores, v_ref[:, cut], plain)

    running[...] = jnp.zeros_like(running)
    for r in range(n_chip - 1):

        @pl.when(r < chip)
        def _():
            remote(
                chip_total, got_total.at[r], tot_send.at[r, 0], tot_recv.at[r], sibling
            ).wait_recv()
            remote(
                chip_state, got_state.at[r], st_send.at[r, 0], st_recv.at[r], sibling
            ).wait_recv()
            kept = jnp.exp(got_total[r][0:1])
            for h in range(heads):
                running[h] = running[h] * kept[:, h : h + 1] + got_state[r, h].astype(jnp.float32)

    @pl.when(core == 1)
    def _():
        kept = jnp.exp(sib_total[0:1])
        for h in range(heads):
            running[h] = running[h] * kept[:, h : h + 1] + sib_state[h].astype(jnp.float32)

    grown = jnp.exp(cumulative)
    for h in range(heads):
        cut = slice(h * DH, (h + 1) * DH)
        state = running[h]
        high = state.astype(jnp.bfloat16)
        low = (state - high.astype(jnp.float32)).astype(jnp.bfloat16)
        carried = jnp.dot(q_ref[:, cut], high, preferred_element_type=jnp.float32) + jnp.dot(
            q_ref[:, cut], low, preferred_element_type=jnp.float32
        )
        whole = raw[:, cut] + grown[:, h : h + 1] * carried
        square = jnp.mean(whole * whole, axis=1, keepdims=True)
        ret[:, cut] = (whole * lax.rsqrt(square + epsilon)).astype(jnp.bfloat16)

    def part_of(s):
        start = pl.multiple_of(s * piece, piece)
        return jnp.dot(ret[...], w_ref[:, pl.ds(start, piece)], preferred_element_type=jnp.float32)

    def part_copy(j):
        return remote(
            send_part.at[j - 1], got_part.at[j - 1], part_send.at[j - 1], part_recv.at[j - 1],
            (lax.rem(sec + j, n_sec), ctx),
        )

    for j in range(1, n_sec):
        send_part[j - 1] = part_of(lax.rem(sec + j, n_sec)).astype(jnp.bfloat16)
        part_copy(j).start()
    summed = part_of(sec)
    for r in range(1, n_ctx):

        @pl.when(r > ctx)
        def _():
            out_ref[r * rows : (r + 1) * rows, :] = jnp.zeros((rows, columns), jnp.bfloat16)

    for j in range(1, n_sec):
        part_copy(j).wait_recv()
        summed += got_part[j - 1].astype(jnp.float32)
    my_rows = pl.ds(pl.multiple_of(ctx * rows, rows), rows)
    my_cut = pl.ds(pl.multiple_of(sec * piece, piece), piece)
    out_ref[my_rows, my_cut] = summed.astype(jnp.bfloat16)

    def z_copy(j):
        spot = out_ref.at[my_rows, my_cut]
        return remote(spot, spot, z_send.at[j - 1], z_recv.at[j - 1], (lax.rem(sec + j, n_sec), ctx))

    for j in range(1, n_sec):
        z_copy(j).start()
    for j in range(1, n_sec):
        z_copy(j).wait_recv()

    def x_copy(r, c):
        spot = out_ref.at[my_rows, c * half : (c + 1) * half]
        return remote(spot, spot, x_send.at[r, c], x_recv.at[ctx], (sec, 2 * r + c))

    def y_copy(d, c, cut, device):
        spot = out_ref.at[d * rows : (d + 1) * rows, cut]
        return remote(spot, spot, y_send.at[d], y_recv.at[d], device)

    for r in range(n_chip - 1, 0, -1):

        @pl.when(r > chip)
        def _():
            for c in range(2):
                x_copy(r, c).start()

    def own_copy():
        spot = out_ref.at[my_rows, :]
        return remote(spot, spot, y_send.at[n_ctx], y_recv.at[n_ctx], sibling)

    @pl.when(core == 0)
    def _():
        own_copy().start()

    my_half = pl.ds(pl.multiple_of(core * half, half), half)
    for d in range(n_ctx - 3, -1, -1):

        @pl.when(d < chip * 2)
        def _():
            spot = out_ref.at[d * rows : (d + 1) * rows, my_half]
            remote(spot, spot, x_send.at[0, 0], x_recv.at[d], sibling).wait_recv()
            y_copy(d, core, my_half, sibling).start()

    other_half = pl.ds(pl.multiple_of((1 - core) * half, half), half)
    for d in range(n_ctx - 2):

        @pl.when(d < chip * 2)
        def _():
            y_copy(d, core, other_half, sibling).wait_recv()
            y_copy(d, core, my_half, sibling).wait_send()

    @pl.when(core == 0)
    def _():
        own_copy().wait_send()
        to_sibling(0).wait_send()
        to_sibling(1).wait_send()

    @pl.when(core == 1)
    def _():
        spot = out_ref.at[pl.ds(pl.multiple_of((ctx - core) * rows, rows), rows), :]
        remote(spot, spot, y_send.at[n_ctx], y_recv.at[n_ctx], sibling).wait_recv()

    for r in range(1, n_chip):

        @pl.when(r > chip)
        def _():
            for c in range(2):
                x_copy(r, c).wait_send()

            @pl.when(core == 1)
            def _():
                for c in range(2):
                    chip_copy(r, c, 0).wait_send()
                    chip_copy(r, c, 1).wait_send()

    for j in range(1, n_sec):
        part_copy(j).wait_send()
        z_copy(j).wait_send()


def shared_cache(ret_query, ret_key, ret_value, gate_log, kv_weight):
    n_sec, n_ctx = lax.axis_size("section"), lax.axis_size("ctx")
    n_chip = n_ctx // 2
    rows, width = ret_query.shape
    heads = width // DH
    columns = kv_weight.shape[1]
    piece = columns // n_sec
    gate = jnp.pad(gate_log, ((0, 0), (0, 128 - heads)))
    turned = jnp.pad(gate_log.T, ((0, 8 - heads), (0, 0)))
    state = pltpu.VMEM((heads, DH, DH), jnp.bfloat16)
    total = pltpu.VMEM((8, 128), jnp.float32)
    dma = pltpu.SemaphoreType.DMA
    vmem = pl.BlockSpec(memory_space=pltpu.VMEM)
    return pl.pallas_call(
        functools.partial(cache_kernel, n_sec, n_ctx),
        out_shape=jax.ShapeDtypeStruct((n_ctx * rows, columns), jnp.bfloat16),
        in_specs=[vmem] * 6,
        out_specs=vmem,
        scratch_shapes=[
            pltpu.VMEM((rows, width), jnp.bfloat16),
            pltpu.VMEM((rows, width), jnp.float32),
            state, total, state, total, state, total,
            pltpu.VMEM((n_chip, heads, DH, DH), jnp.bfloat16),
            pltpu.VMEM((n_chip, 8, 128), jnp.float32),
            pltpu.VMEM((heads, DH, DH), jnp.float32),
            pltpu.VMEM((n_sec - 1, rows, piece), jnp.bfloat16),
            pltpu.VMEM((n_sec - 1, rows, piece), jnp.bfloat16),
            dma((2,)), dma((2,)),
            dma((n_chip, 2)), dma((n_chip,)),
            dma((n_chip, 2)), dma((n_chip,)),
            dma((n_sec - 1,)), dma((n_sec - 1,)),
            dma((n_sec - 1,)), dma((n_sec - 1,)),
            dma((n_chip, 2)), dma((n_ctx,)),
            dma((n_ctx + 1,)), dma((n_ctx + 1,)),
        ],
        compiler_params=pltpu.CompilerParams(
            collective_id=0, has_side_effects=True, vmem_limit_bytes=LIMIT
        ),
    )(ret_query, ret_key, ret_value, gate, turned, kv_weight)


def gradient_kernel(
    n_sec,
    n_ctx,
    kg_ref,
    vg_ref,
    out_ref,
    from_sib,
    send_chip,
    got_chip,
    kept,
    send_part,
    got_part,
    final,
    sib_send,
    sib_recv,
    chip_send,
    chip_recv,
    part_send,
    part_recv,
    all_send,
    all_recv,
):
    sec, ctx = lax.axis_index("section"), lax.axis_index("ctx")
    chip, core = lax.div(ctx, 2), lax.rem(ctx, 2)
    n_chip = n_ctx // 2
    sibling = (sec, chip * 2 + 1 - core)
    rows = out_ref.shape[0]
    pair = 2 * rows
    half = kg_ref.shape[1]
    piece = half // n_sec

    others = [(lax.rem(sec + j, n_sec), chip * 2 + lax.rem(core + c, 2), j, c)
              for j in range(n_sec) for c in range(2) if j or c]
    greet(
        [(s, d) for s, d, _, _ in others]
        + [(sec, lax.rem(ctx + 2 * i, n_ctx)) for i in range(1, n_chip)]
    )

    def sib_copy(r, ref):
        return remote(
            ref.at[r * pair : (r + 1) * pair, :], from_sib.at[r], sib_send.at[r], sib_recv.at[r],
            sibling,
        )

    for r in range(n_chip):

        @pl.when(jnp.logical_and(r <= chip, core == 0))
        def _():
            sib_copy(r, vg_ref).start()

        @pl.when(jnp.logical_and(r <= chip, core == 1))
        def _():
            sib_copy(r, kg_ref).start()

    def chip_copy(r):
        return remote(
            send_chip.at[r], got_chip.at[chip], chip_send.at[r], chip_recv.at[chip],
            (sec, 2 * r + core),
        )

    for r in range(n_chip):

        @pl.when(r <= chip)
        def _():
            sib_copy(r, kg_ref).wait_recv()
            cut = slice(r * pair, (r + 1) * pair)

            @pl.when(core == 0)
            def _():
                kept[...] = kg_ref[cut, :].astype(jnp.float32) + from_sib[r].astype(jnp.float32)

            @pl.when(core == 1)
            def _():
                kept[...] = vg_ref[cut, :].astype(jnp.float32) + from_sib[r].astype(jnp.float32)

            @pl.when(r < chip)
            def _():
                send_chip[r] = kept[...].astype(jnp.bfloat16)
                chip_copy(r).start()

    for r in range(1, n_chip):

        @pl.when(r > chip)
        def _():
            remote(
                send_chip.at[r], got_chip.at[r], chip_send.at[r], chip_recv.at[r], sibling
            ).wait_recv()
            kept[...] += got_chip[r].astype(jnp.float32)

    def part_copy(j):
        return remote(
            send_part.at[j - 1], got_part.at[j - 1], part_send.at[j - 1], part_recv.at[j - 1],
            (lax.rem(sec + j, n_sec), ctx),
        )

    def cut_of(s):
        return pl.ds(pl.multiple_of(s * piece, piece), piece)

    for j in range(1, n_sec):
        send_part[j - 1] = kept[:, cut_of(lax.rem(sec + j, n_sec))].astype(jnp.bfloat16)
        part_copy(j).start()
    summed = kept[:, cut_of(sec)]
    for j in range(1, n_sec):
        part_copy(j).wait_recv()
        summed += got_part[j - 1].astype(jnp.float32)
    final[...] = summed.astype(jnp.bfloat16)
    place = pl.ds(pl.multiple_of(core * half + sec * piece, piece), piece)

    def all_copy(s, d, j, c):
        part = pl.ds(pl.multiple_of(lax.rem(core + c, 2) * rows, rows), rows)
        return remote(
            final.at[part, :], out_ref.at[:, place], all_send.at[j, c], all_recv.at[j, c], (s, d)
        )

    for s, d, j, c in others:
        all_copy(s, d, j, c).start()
    out_ref[:, place] = final[pl.ds(pl.multiple_of(core * rows, rows), rows), :]
    for s, d, j, c in others:
        all_copy(s, d, j, c).wait_recv()
    for s, d, j, c in others:
        all_copy(s, d, j, c).wait_send()
    for j in range(1, n_sec):
        part_copy(j).wait_send()
    for r in range(n_chip):

        @pl.when(r <= chip)
        def _():
            sib_copy(r, kg_ref).wait_send()

        @pl.when(r < chip)
        def _():
            chip_copy(r).wait_send()


def summed_gradient(key_grad, value_grad):
    n_sec, n_ctx = lax.axis_size("section"), lax.axis_size("ctx")
    n_chip = n_ctx // 2
    total, half = key_grad.shape
    rows = total // n_ctx
    pair = 2 * rows
    piece = half // n_sec
    dma = pltpu.SemaphoreType.DMA
    vmem = pl.BlockSpec(memory_space=pltpu.VMEM)
    chips = pltpu.VMEM((n_chip, pair, half), jnp.bfloat16)
    parts = pltpu.VMEM((n_sec - 1, pair, piece), jnp.bfloat16)
    return pl.pallas_call(
        functools.partial(gradient_kernel, n_sec, n_ctx),
        out_shape=jax.ShapeDtypeStruct((rows, 2 * half), jnp.bfloat16),
        in_specs=[vmem] * 2,
        out_specs=vmem,
        scratch_shapes=[
            chips, chips, chips,
            pltpu.VMEM((pair, half), jnp.float32),
            parts, parts,
            pltpu.VMEM((pair, piece), jnp.bfloat16),
            dma((n_chip,)), dma((n_chip,)),
            dma((n_chip,)), dma((n_chip,)),
            dma((n_sec - 1,)), dma((n_sec - 1,)),
            dma((n_sec, 2)), dma((n_sec, 2)),
        ],
        compiler_params=pltpu.CompilerParams(
            collective_id=1, has_side_effects=True, vmem_limit_bytes=LIMIT
        ),
    )(key_grad, value_grad)


def attention_kernel(ctx_ref, q_ref, g_ref, k_ref, v_ref, att_ref, qg_ref, kg_ref, vg_ref):
    layer_count, row_count, width = q_ref.shape
    group = width // DH
    total = k_ref.shape[0]
    columns = group * row_count
    scale = 1.0 / math.sqrt(DH)
    keys = k_ref[...]
    values = v_ref[...]
    key_place = lax.broadcasted_iota(jnp.int32, (total, row_count), 0)
    row_place = ctx_ref[0] * row_count + lax.broadcasted_iota(jnp.int32, (total, row_count), 1)
    visible = jnp.concatenate([jnp.where(key_place <= row_place, 0.0, -jnp.inf)] * group, axis=1)

    def stacked(ref, layer):
        return jnp.concatenate(
            [ref[layer, :, j * DH : (j + 1) * DH] for j in range(group)], axis=0
        )

    def spread(ref, layer, rows):
        for j in range(group):
            ref[layer, :, j * DH : (j + 1) * DH] = rows[j * row_count : (j + 1) * row_count]

    key_grad = jnp.zeros((total, DH), jnp.float32)
    value_grad = jnp.zeros((total, DH), jnp.float32)
    for layer in range(layer_count):
        queries = stacked(q_ref, layer)
        grads = stacked(g_ref, layer)
        scores = lax.dot_general(
            keys, queries, (((1,), (1,)), ((), ())), preferred_element_type=jnp.float32
        )
        scores = scores * scale + visible
        top = jnp.max(scores, axis=0, keepdims=True)
        soft = jnp.exp(scores - top)
        soft = soft * (1.0 / jnp.sum(soft, axis=0, keepdims=True))
        low = soft.astype(jnp.bfloat16)
        mixed = lax.dot_general(
            low, values, (((0,), (0,)), ((), ())), preferred_element_type=jnp.float32
        ).astype(jnp.bfloat16)
        spread(att_ref, layer, mixed)
        product = grads.astype(jnp.float32) * mixed.astype(jnp.float32)
        delta = jnp.sum(product.T, axis=0, keepdims=True)
        prob_grad = lax.dot_general(
            values, grads, (((1,), (1,)), ((), ())), preferred_element_type=jnp.float32
        )
        score_grad = (soft * (prob_grad - delta) * scale).astype(jnp.bfloat16)
        query_grad = lax.dot_general(
            score_grad, keys, (((0,), (0,)), ((), ())), preferred_element_type=jnp.float32
        )
        spread(qg_ref, layer, query_grad.astype(jnp.bfloat16))
        key_grad += jnp.dot(score_grad, queries, preferred_element_type=jnp.float32)
        value_grad += jnp.dot(low, grads, preferred_element_type=jnp.float32)
    kg_ref[...] = key_grad.astype(kg_ref.dtype)
    vg_ref[...] = value_grad.astype(vg_ref.dtype)


def cross_attention(queries, cotangent, full_cache, place):
    layer_count, row_count, model_width = queries.shape
    total, cache_width = full_cache.shape
    kv_heads = cache_width // 2 // DH
    width = model_width // kv_heads
    rows = pl.BlockSpec((layer_count, row_count, width), lambda h, c: (0, 0, h))
    cut = pl.BlockSpec((total, DH), lambda h, c: (0, h))
    cut_values = pl.BlockSpec((total, DH), lambda h, c: (0, kv_heads + h))
    half = jax.ShapeDtypeStruct((total, cache_width // 2), jnp.bfloat16)
    return pl.pallas_call(
        attention_kernel,
        grid_spec=pltpu.PrefetchScalarGridSpec(
            num_scalar_prefetch=1,
            grid=(kv_heads,),
            in_specs=[rows, rows, cut, cut_values],
            out_specs=[rows, rows, cut, cut],
        ),
        out_shape=[
            jax.ShapeDtypeStruct(queries.shape, jnp.bfloat16),
            jax.ShapeDtypeStruct(queries.shape, jnp.bfloat16),
            half,
            half,
        ],
        compiler_params=pltpu.CompilerParams(vmem_limit_bytes=LIMIT),
    )(place, queries, cotangent, full_cache, full_cache)


def body(queries, cotangent, ret_query, ret_key, ret_value, gate_log, kv_weight):
    full_cache = shared_cache(ret_query, ret_key, ret_value, gate_log, kv_weight)
    place = lax.axis_index("ctx").reshape(1)
    attended_all, grad_rows_all, key_grad, value_grad = cross_attention(
        queries, cotangent, full_cache, place
    )
    cache_grad = summed_gradient(key_grad, value_grad)
    retention_grad = jnp.einsum(
        "rw,cw->rc", cache_grad, kv_weight, preferred_element_type=jnp.float32
    ).astype(jnp.bfloat16)
    return (attended_all, grad_rows_all, retention_grad)


def solution(mesh):
    return jax.shard_map(
        body,
        mesh=mesh,
        in_specs=(
            P("section", "ctx", None),
            P("section", "ctx", None),
            P("ctx", "section"),
            P("ctx", "section"),
            P("ctx", "section"),
            P("ctx", "section"),
            P("section", None),
        ),
        out_specs=(P("section", "ctx", None), P("section", "ctx", None), P("ctx", "section")),
        check_vma=False,
    )
```

```python
import functools
import math

import jax
import jax.numpy as jnp
from jax import lax
from jax.experimental import pallas as pl
from jax.experimental.pallas import tpu as pltpu
from jax.sharding import PartitionSpec as P

DH = 128


epsilon = 1e-06
highest = lax.Precision.HIGHEST

MESH = pl.DeviceIdType.MESH
LIMIT = 56 * 1024 * 1024


def greet(peers):
    barrier = pltpu.get_barrier_semaphore()
    for peer in peers:
        pl.semaphore_signal(barrier, inc=1, device_id=peer, device_id_type=MESH)
    pl.semaphore_wait(barrier, len(peers))


def remote(source, target, send_sem, recv_sem, device):
    return pltpu.make_async_remote_copy(
        src_ref=source,
        dst_ref=target,
        send_sem=send_sem,
        recv_sem=recv_sem,
        device_id=device,
        device_id_type=MESH,
    )


def two_part_dot(wide, narrow, dims):
    high = wide.astype(jnp.bfloat16)
    low = (wide - high.astype(jnp.float32)).astype(jnp.bfloat16)
    return lax.dot_general(
        high, narrow, dims, preferred_element_type=jnp.float32
    ) + lax.dot_general(low, narrow, dims, preferred_element_type=jnp.float32)


def cache_kernel(
    n_sec,
    n_ctx,
    q_ref,
    k_ref,
    v_ref,
    gate_ref,
    turned_ref,
    w_ref,
    out_ref,
    ret,
    raw,
    own_state,
    own_total,
    sib_state,
    sib_total,
    chip_state,
    chip_total,
    got_state,
    got_total,
    running,
    send_part,
    got_part,
    sib_send,
    sib_recv,
    st_send,
    st_recv,
    tot_send,
    tot_recv,
    part_send,
    part_recv,
    z_send,
    z_recv,
    x_send,
    x_recv,
    y_send,
    y_recv,
):
    sec, ctx = lax.axis_index("section"), lax.axis_index("ctx")
    chip, core = lax.div(ctx, 2), lax.rem(ctx, 2)
    n_chip = n_ctx // 2
    sibling = (sec, chip * 2 + 1 - core)
    rows, width = q_ref.shape
    heads = width // DH
    columns = out_ref.shape[1]
    piece = columns // n_sec
    half = columns // 2
    row_dims = (((0,), (0,)), ((), ()))
    plain = (((1,), (0,)), ((), ()))
    last_dims = (((1,), (1,)), ((), ()))

    greet(
        [(lax.rem(sec + j, n_sec), ctx) for j in range(1, n_sec)]
        + [(sec, lax.rem(ctx + j, n_ctx)) for j in range(1, n_ctx)]
    )

    first = lax.broadcasted_iota(jnp.int32, (rows, rows), 0)
    second = lax.broadcasted_iota(jnp.int32, (rows, rows), 1)
    causal = first >= second
    cumulative = jnp.dot(
        causal.astype(jnp.float32), gate_ref[...], precision=highest,
        preferred_element_type=jnp.float32,
    )
    turned = jnp.dot(
        turned_ref[...], (first <= second).astype(jnp.float32), precision=highest,
        preferred_element_type=jnp.float32,
    )
    total = cumulative[rows - 1 : rows]
    own_total[...] = jnp.broadcast_to(total, own_total.shape)
    tail = jnp.exp(total - cumulative)
    for h in range(heads):
        cut = slice(h * DH, (h + 1) * DH)
        decayed = k_ref[:, cut].astype(jnp.float32) * tail[:, h : h + 1]
        own_state[h] = two_part_dot(decayed, v_ref[:, cut], row_dims).astype(jnp.bfloat16)

    def to_sibling(index):
        pair = ((own_state, sib_state), (own_total, sib_total))[index]
        return remote(*pair, sib_send.at[index], sib_recv.at[index], sibling)

    @pl.when(core == 0)
    def _():
        to_sibling(0).start()
        to_sibling(1).start()

    def chip_copy(r, c, index):
        if index == 0:
            return remote(
                chip_state, got_state.at[chip], st_send.at[r, c], st_recv.at[chip], (sec, 2 * r + c)
            )
        return remote(
            chip_total, got_total.at[chip], tot_send.at[r, c], tot_recv.at[chip], (sec, 2 * r + c)
        )

    @pl.when(core == 1)
    def _():
        to_sibling(0).wait_recv()
        to_sibling(1).wait_recv()
        chip_total[...] = own_total[...] + sib_total[...]
        kept = jnp.exp(total)
        for h in range(heads):
            chip_state[h] = (
                sib_state[h].astype(jnp.float32) * kept[:, h : h + 1]
                + own_state[h].astype(jnp.float32)
            ).astype(jnp.bfloat16)
        for r in range(n_chip - 1, 0, -1):

            @pl.when(chip < r)
            def _():
                for c in range(2):
                    chip_copy(r, c, 1).start()
                    chip_copy(r, c, 0).start()

    for h in range(heads):
        cut = slice(h * DH, (h + 1) * DH)
        spread = cumulative[:, h : h + 1] - turned[h : h + 1, :]
        weights = jnp.exp(jnp.where(causal, spread, -jnp.inf))
        scores = lax.dot_general(
            q_ref[:, cut], k_ref[:, cut], last_dims, preferred_element_type=jnp.float32
        )
        raw[:, cut] = two_part_dot(weights * scores, v_ref[:, cut], plain)

    running[...] = jnp.zeros_like(running)
    for r in range(n_chip - 1):

        @pl.when(r < chip)
        def _():
            remote(
                chip_total, got_total.at[r], tot_send.at[r, 0], tot_recv.at[r], sibling
            ).wait_recv()
            remote(
                chip_state, got_state.at[r], st_send.at[r, 0], st_recv.at[r], sibling
            ).wait_recv()
            kept = jnp.exp(got_total[r][0:1])
            for h in range(heads):
                running[h] = running[h] * kept[:, h : h + 1] + got_state[r, h].astype(jnp.float32)

    @pl.when(core == 1)
    def _():
        kept = jnp.exp(sib_total[0:1])
        for h in range(heads):
            running[h] = running[h] * kept[:, h : h + 1] + sib_state[h].astype(jnp.float32)

    grown = jnp.exp(cumulative)
    for h in range(heads):
        cut = slice(h * DH, (h + 1) * DH)
        state = running[h]
        high = state.astype(jnp.bfloat16)
        low = (state - high.astype(jnp.float32)).astype(jnp.bfloat16)
        carried = jnp.dot(q_ref[:, cut], high, preferred_element_type=jnp.float32) + jnp.dot(
            q_ref[:, cut], low, preferred_element_type=jnp.float32
        )
        whole = raw[:, cut] + grown[:, h : h + 1] * carried
        square = jnp.mean(whole * whole, axis=1, keepdims=True)
        ret[:, cut] = (whole * lax.rsqrt(square + epsilon)).astype(jnp.bfloat16)

    def part_of(s):
        start = pl.multiple_of(s * piece, piece)
        return jnp.dot(ret[...], w_ref[:, pl.ds(start, piece)], preferred_element_type=jnp.float32)

    def part_copy(j):
        return remote(
            send_part.at[j - 1], got_part.at[j - 1], part_send.at[j - 1], part_recv.at[j - 1],
            (lax.rem(sec + j, n_sec), ctx),
        )

    for j in range(1, n_sec):
        send_part[j - 1] = part_of(lax.rem(sec + j, n_sec)).astype(jnp.bfloat16)
        part_copy(j).start()
    summed = part_of(sec)
    for r in range(1, n_ctx):

        @pl.when(r > ctx)
        def _():
            out_ref[r * rows : (r + 1) * rows, :] = jnp.zeros((rows, columns), jnp.bfloat16)

    for j in range(1, n_sec):
        part_copy(j).wait_recv()
        summed += got_part[j - 1].astype(jnp.float32)
    my_rows = pl.ds(pl.multiple_of(ctx * rows, rows), rows)
    my_cut = pl.ds(pl.multiple_of(sec * piece, piece), piece)
    out_ref[my_rows, my_cut] = summed.astype(jnp.bfloat16)

    def z_copy(j):
        spot = out_ref.at[my_rows, my_cut]
        return remote(spot, spot, z_send.at[j - 1], z_recv.at[j - 1], (lax.rem(sec + j, n_sec), ctx))

    for j in range(1, n_sec):
        z_copy(j).start()
    for j in range(1, n_sec):
        z_copy(j).wait_recv()

    def x_copy(r, c):
        spot = out_ref.at[my_rows, c * half : (c + 1) * half]
        return remote(spot, spot, x_send.at[r, c], x_recv.at[ctx], (sec, 2 * r + c))

    def y_copy(d, c, cut, device):
        spot = out_ref.at[d * rows : (d + 1) * rows, cut]
        return remote(spot, spot, y_send.at[d], y_recv.at[d], device)

    for r in range(n_chip - 1, 0, -1):

        @pl.when(r > chip)
        def _():
            for c in range(2):
                x_copy(r, c).start()

    def own_copy():
        spot = out_ref.at[my_rows, :]
        return remote(spot, spot, y_send.at[n_ctx], y_recv.at[n_ctx], sibling)

    @pl.when(core == 0)
    def _():
        own_copy().start()

    my_half = pl.ds(pl.multiple_of(core * half, half), half)
    for d in range(n_ctx - 3, -1, -1):

        @pl.when(d < chip * 2)
        def _():
            spot = out_ref.at[d * rows : (d + 1) * rows, my_half]
            remote(spot, spot, x_send.at[0, 0], x_recv.at[d], sibling).wait_recv()
            y_copy(d, core, my_half, sibling).start()

    other_half = pl.ds(pl.multiple_of((1 - core) * half, half), half)
    for d in range(n_ctx - 2):

        @pl.when(d < chip * 2)
        def _():
            y_copy(d, core, other_half, sibling).wait_recv()
            y_copy(d, core, my_half, sibling).wait_send()

    @pl.when(core == 0)
    def _():
        own_copy().wait_send()
        to_sibling(0).wait_send()
        to_sibling(1).wait_send()

    @pl.when(core == 1)
    def _():
        spot = out_ref.at[pl.ds(pl.multiple_of((ctx - core) * rows, rows), rows), :]
        remote(spot, spot, y_send.at[n_ctx], y_recv.at[n_ctx], sibling).wait_recv()

    for r in range(1, n_chip):

        @pl.when(r > chip)
        def _():
            for c in range(2):
                x_copy(r, c).wait_send()

            @pl.when(core == 1)
            def _():
                for c in range(2):
                    chip_copy(r, c, 0).wait_send()
                    chip_copy(r, c, 1).wait_send()

    for j in range(1, n_sec):
        part_copy(j).wait_send()
        z_copy(j).wait_send()


def shared_cache(ret_query, ret_key, ret_value, gate_log, kv_weight):
    n_sec, n_ctx = lax.axis_size("section"), lax.axis_size("ctx")
    n_chip = n_ctx // 2
    rows, width = ret_query.shape
    heads = width // DH
    columns = kv_weight.shape[1]
    piece = columns // n_sec
    gate = jnp.pad(gate_log, ((0, 0), (0, 128 - heads)))
    turned = jnp.pad(gate_log.T, ((0, 8 - heads), (0, 0)))
    state = pltpu.VMEM((heads, DH, DH), jnp.bfloat16)
    total = pltpu.VMEM((8, 128), jnp.float32)
    dma = pltpu.SemaphoreType.DMA
    vmem = pl.BlockSpec(memory_space=pltpu.VMEM)
    return pl.pallas_call(
        functools.partial(cache_kernel, n_sec, n_ctx),
        out_shape=jax.ShapeDtypeStruct((n_ctx * rows, columns), jnp.bfloat16),
        in_specs=[vmem] * 6,
        out_specs=vmem,
        scratch_shapes=[
            pltpu.VMEM((rows, width), jnp.bfloat16),
            pltpu.VMEM((rows, width), jnp.float32),
            state, total, state, total, state, total,
            pltpu.VMEM((n_chip, heads, DH, DH), jnp.bfloat16),
            pltpu.VMEM((n_chip, 8, 128), jnp.float32),
            pltpu.VMEM((heads, DH, DH), jnp.float32),
            pltpu.VMEM((n_sec - 1, rows, piece), jnp.bfloat16),
            pltpu.VMEM((n_sec - 1, rows, piece), jnp.bfloat16),
            dma((2,)), dma((2,)),
            dma((n_chip, 2)), dma((n_chip,)),
            dma((n_chip, 2)), dma((n_chip,)),
            dma((n_sec - 1,)), dma((n_sec - 1,)),
            dma((n_sec - 1,)), dma((n_sec - 1,)),
            dma((n_chip, 2)), dma((n_ctx,)),
            dma((n_ctx + 1,)), dma((n_ctx + 1,)),
        ],
        compiler_params=pltpu.CompilerParams(
            collective_id=0, has_side_effects=True, vmem_limit_bytes=LIMIT
        ),
    )(ret_query, ret_key, ret_value, gate, turned, kv_weight)


def attention_kernel(
    n_sec,
    n_ctx,
    q_ref,
    g_ref,
    k_ref,
    v_ref,
    att_ref,
    qg_ref,
    out_ref,
    send_sib,
    keep,
    from_sib,
    got_chip,
    kept,
    send_part,
    got_part,
    final,
    gathered,
    sib_send,
    sib_recv,
    chip_send,
    chip_recv,
    part_send,
    part_recv,
    all_send,
    all_recv,
):
    sec, ctx = lax.axis_index("section"), lax.axis_index("ctx")
    chip, core = lax.div(ctx, 2), lax.rem(ctx, 2)
    n_chip = n_ctx // 2
    sibling = (sec, chip * 2 + 1 - core)
    step = pl.program_id(0)
    kv_heads = kept.shape[0]
    part_heads = kv_heads // n_sec
    layer_count, row_count, width = q_ref.shape
    group = width // DH
    total = k_ref.shape[0]
    pair = 2 * row_count
    scale = 1.0 / math.sqrt(DH)

    others = [
        (lax.rem(sec + j, n_sec), chip * 2 + lax.rem(core + c, 2), j, c)
        for j in range(n_sec)
        for c in range(2)
        if j or c
    ]

    @pl.when(step == 0)
    def _():
        greet(
            [(s, d) for s, d, _, _ in others]
            + [(sec, lax.rem(ctx + 2 * i, n_ctx)) for i in range(1, n_chip)]
        )

    def sib_copy(h):
        return remote(send_sib.at[h], from_sib.at[h], sib_send.at[h], sib_recv.at[h], sibling)

    def chip_copy(r, h):
        return remote(
            keep.at[h, r * pair : (r + 1) * pair, :],
            got_chip.at[chip, h],
            chip_send.at[r, h],
            chip_recv.at[chip, h],
            (sec, 2 * r + core),
        )

    def pass_on(h):
        sib_copy(h).wait_recv()
        mine = pl.ds(pl.multiple_of(chip * pair, pair), pair)
        kept[h] = keep[h, mine, :].astype(jnp.float32) + from_sib[h, mine, :].astype(jnp.float32)
        for r in range(n_chip - 1):

            @pl.when(r < chip)
            def _():
                cut = slice(r * pair, (r + 1) * pair)
                keep[h, cut, :] = (
                    keep[h, cut, :].astype(jnp.float32) + from_sib[h, cut, :].astype(jnp.float32)
                ).astype(jnp.bfloat16)
                chip_copy(r, h).start()

    keys = k_ref[...]
    values = v_ref[...]
    key_place = lax.broadcasted_iota(jnp.int32, (total, row_count), 0)
    row_place = ctx * row_count + lax.broadcasted_iota(jnp.int32, (total, row_count), 1)
    visible = jnp.concatenate([jnp.where(key_place <= row_place, 0.0, -jnp.inf)] * group, axis=1)

    def stacked(ref, layer):
        return jnp.concatenate(
            [ref[layer, :, j * DH : (j + 1) * DH] for j in range(group)], axis=0
        )

    def spread(ref, layer, rows):
        for j in range(group):
            ref[layer, :, j * DH : (j + 1) * DH] = rows[j * row_count : (j + 1) * row_count]

    key_grad = jnp.zeros((total, DH), jnp.float32)
    value_grad = jnp.zeros((total, DH), jnp.float32)
    for layer in range(layer_count):
        queries = stacked(q_ref, layer)
        grads = stacked(g_ref, layer)
        scores = lax.dot_general(
            keys, queries, (((1,), (1,)), ((), ())), preferred_element_type=jnp.float32
        )
        scores = scores * scale + visible
        top = jnp.max(scores, axis=0, keepdims=True)
        soft = jnp.exp(scores - top)
        soft = soft * (1.0 / jnp.sum(soft, axis=0, keepdims=True))
        low = soft.astype(jnp.bfloat16)
        mixed = lax.dot_general(
            low, values, (((0,), (0,)), ((), ())), preferred_element_type=jnp.float32
        ).astype(jnp.bfloat16)
        spread(att_ref, layer, mixed)
        product = grads.astype(jnp.float32) * mixed.astype(jnp.float32)
        delta = jnp.sum(product.T, axis=0, keepdims=True)
        prob_grad = lax.dot_general(
            values, grads, (((1,), (1,)), ((), ())), preferred_element_type=jnp.float32
        )
        score_grad = (soft * (prob_grad - delta) * scale).astype(jnp.bfloat16)
        query_grad = lax.dot_general(
            score_grad, keys, (((0,), (0,)), ((), ())), preferred_element_type=jnp.float32
        )
        spread(qg_ref, layer, query_grad.astype(jnp.bfloat16))
        key_grad += jnp.dot(score_grad, queries, preferred_element_type=jnp.float32)
        value_grad += jnp.dot(low, grads, preferred_element_type=jnp.float32)
        if layer == 0:

            @pl.when(step > 0)
            def _():
                pass_on(step - 1)

    key_low = key_grad.astype(jnp.bfloat16)
    value_low = value_grad.astype(jnp.bfloat16)

    @pl.when(core == 0)
    def _():
        keep[step] = key_low
        send_sib[step] = value_low

    @pl.when(core == 1)
    def _():
        keep[step] = value_low
        send_sib[step] = key_low

    sib_copy(step).start()

    def part_copy(j):
        return remote(
            send_part.at[j - 1],
            got_part.at[j - 1],
            part_send.at[j - 1],
            part_recv.at[j - 1],
            (lax.rem(sec + j, n_sec), ctx),
        )

    piece = part_heads * DH
    place = pl.ds(pl.multiple_of(core * kv_heads * DH + sec * piece, piece), piece)

    def all_copy(s, d, j, c):
        part = pl.ds(pl.multiple_of(lax.rem(core + c, 2) * row_count, row_count), row_count)
        return remote(
            final.at[part, :], gathered.at[:, place], all_send.at[j, c], all_recv.at[j, c], (s, d)
        )

    @pl.when(step == kv_heads - 1)
    def _():
        pass_on(kv_heads - 1)
        for h in range(kv_heads):
            for r in range(1, n_chip):

                @pl.when(r > chip)
                def _():
                    remote(
                        keep.at[h, 0:pair, :],
                        got_chip.at[r, h],
                        chip_send.at[r, h],
                        chip_recv.at[r, h],
                        sibling,
                    ).wait_recv()
                    kept[h] += got_chip[r, h].astype(jnp.float32)

        for j in range(1, n_sec):
            first = lax.rem(sec + j, n_sec) * part_heads
            for i in range(part_heads):
                send_part[j - 1, :, i * DH : (i + 1) * DH] = kept[first + i].astype(jnp.bfloat16)
            part_copy(j).start()
        for j in range(1, n_sec):
            part_copy(j).wait_recv()
        for i in range(part_heads):
            cut = slice(i * DH, (i + 1) * DH)
            summed = kept[sec * part_heads + i]
            for j in range(1, n_sec):
                summed += got_part[j - 1, :, cut].astype(jnp.float32)
            final[:, cut] = summed.astype(jnp.bfloat16)
        for s, d, j, c in others:
            all_copy(s, d, j, c).start()
        own = pl.ds(pl.multiple_of(core * row_count, row_count), row_count)
        gathered[:, place] = final[own, :]
        for s, d, j, c in others:
            all_copy(s, d, j, c).wait_recv()
        out_ref[...] = gathered[...]
        for s, d, j, c in others:
            all_copy(s, d, j, c).wait_send()
        for j in range(1, n_sec):
            part_copy(j).wait_send()
        for h in range(kv_heads):
            sib_copy(h).wait_send()
            for r in range(n_chip - 1):

                @pl.when(r < chip)
                def _():
                    chip_copy(r, h).wait_send()


def cross_attention(queries, cotangent, full_cache):
    n_sec, n_ctx = lax.axis_size("section"), lax.axis_size("ctx")
    n_chip = n_ctx // 2
    layer_count, row_count, model_width = queries.shape
    total, cache_width = full_cache.shape
    kv_heads = cache_width // 2 // DH
    width = model_width // kv_heads
    pair = 2 * row_count
    piece = kv_heads // n_sec * DH
    rows = pl.BlockSpec((layer_count, row_count, width), lambda h: (0, 0, h))
    cut = pl.BlockSpec((total, DH), lambda h: (0, h))
    cut_values = pl.BlockSpec((total, DH), lambda h: (0, kv_heads + h))
    dma = pltpu.SemaphoreType.DMA
    per_head = pltpu.VMEM((kv_heads, total, DH), jnp.bfloat16)
    parts = pltpu.VMEM((n_sec - 1, pair, piece), jnp.bfloat16)
    return pl.pallas_call(
        functools.partial(attention_kernel, n_sec, n_ctx),
        grid=(kv_heads,),
        in_specs=[rows, rows, cut, cut_values],
        out_specs=[rows, rows, pl.BlockSpec((row_count, cache_width), lambda h: (0, 0))],
        out_shape=[
            jax.ShapeDtypeStruct(queries.shape, jnp.bfloat16),
            jax.ShapeDtypeStruct(queries.shape, jnp.bfloat16),
            jax.ShapeDtypeStruct((row_count, cache_width), jnp.bfloat16),
        ],
        scratch_shapes=[
            per_head, per_head, per_head,
            pltpu.VMEM((n_chip, kv_heads, pair, DH), jnp.bfloat16),
            pltpu.VMEM((kv_heads, pair, DH), jnp.float32),
            parts, parts,
            pltpu.VMEM((pair, piece), jnp.bfloat16),
            pltpu.VMEM((row_count, cache_width), jnp.bfloat16),
            dma((kv_heads,)), dma((kv_heads,)),
            dma((n_chip, kv_heads)), dma((n_chip, kv_heads)),
            dma((n_sec - 1,)), dma((n_sec - 1,)),
            dma((n_sec, 2)), dma((n_sec, 2)),
        ],
        compiler_params=pltpu.CompilerParams(
            collective_id=1, has_side_effects=True, vmem_limit_bytes=LIMIT
        ),
    )(queries, cotangent, full_cache, full_cache)


def body(queries, cotangent, ret_query, ret_key, ret_value, gate_log, kv_weight):
    full_cache = shared_cache(ret_query, ret_key, ret_value, gate_log, kv_weight)
    attended_all, grad_rows_all, cache_grad = cross_attention(queries, cotangent, full_cache)
    retention_grad = jnp.einsum(
        "rw,cw->rc", cache_grad, kv_weight, preferred_element_type=jnp.float32
    ).astype(jnp.bfloat16)
    return (attended_all, grad_rows_all, retention_grad)


def solution(mesh):
    return jax.shard_map(
        body,
        mesh=mesh,
        in_specs=(
            P("section", "ctx", None),
            P("section", "ctx", None),
            P("ctx", "section"),
            P("ctx", "section"),
            P("ctx", "section"),
            P("ctx", "section"),
            P("section", None),
        ),
        out_specs=(P("section", "ctx", None), P("section", "ctx", None), P("ctx", "section")),
        check_vma=False,
    )
```

```python
import functools
import math

import jax
import jax.numpy as jnp
from jax import lax
from jax.experimental import pallas as pl
from jax.experimental.pallas import tpu as pltpu
from jax.sharding import PartitionSpec as P

DH = 128


epsilon = 1e-06
highest = lax.Precision.HIGHEST

MESH = pl.DeviceIdType.MESH
LIMIT = 56 * 1024 * 1024


def greet(peers):
    barrier = pltpu.get_barrier_semaphore()
    for peer in peers:
        pl.semaphore_signal(barrier, inc=1, device_id=peer, device_id_type=MESH)
    pl.semaphore_wait(barrier, len(peers))


def remote(source, target, send_sem, recv_sem, device):
    return pltpu.make_async_remote_copy(
        src_ref=source,
        dst_ref=target,
        send_sem=send_sem,
        recv_sem=recv_sem,
        device_id=device,
        device_id_type=MESH,
    )


def two_part_dot(wide, narrow, dims):
    high = wide.astype(jnp.bfloat16)
    low = (wide - high.astype(jnp.float32)).astype(jnp.bfloat16)
    return lax.dot_general(
        high, narrow, dims, preferred_element_type=jnp.float32
    ) + lax.dot_general(low, narrow, dims, preferred_element_type=jnp.float32)


def cache_kernel(
    n_sec,
    n_ctx,
    q_ref,
    k_ref,
    v_ref,
    gate_ref,
    turned_ref,
    w_ref,
    out_ref,
    ret,
    raw,
    own_state,
    own_total,
    sib_state,
    sib_total,
    chip_state,
    chip_total,
    got_state,
    got_total,
    running,
    send_part,
    got_part,
    sib_send,
    sib_recv,
    st_send,
    st_recv,
    tot_send,
    tot_recv,
    part_send,
    part_recv,
    z_send,
    z_recv,
    x_send,
    x_recv,
    y_send,
    y_recv,
):
    sec, ctx = lax.axis_index("section"), lax.axis_index("ctx")
    chip, core = lax.div(ctx, 2), lax.rem(ctx, 2)
    n_chip = n_ctx // 2
    sibling = (sec, chip * 2 + 1 - core)
    rows, width = q_ref.shape
    heads = width // DH
    columns = out_ref.shape[1]
    piece = columns // n_sec
    row_dims = (((0,), (0,)), ((), ()))
    plain = (((1,), (0,)), ((), ()))
    last_dims = (((1,), (1,)), ((), ()))

    greet(
        [(lax.rem(sec + j, n_sec), ctx) for j in range(1, n_sec)]
        + [(sec, lax.rem(ctx + j, n_ctx)) for j in range(1, n_ctx)]
    )

    first = lax.broadcasted_iota(jnp.int32, (rows, rows), 0)
    second = lax.broadcasted_iota(jnp.int32, (rows, rows), 1)
    causal = first >= second
    cumulative = jnp.dot(
        causal.astype(jnp.float32), gate_ref[...], precision=highest,
        preferred_element_type=jnp.float32,
    )
    turned = jnp.dot(
        turned_ref[...], (first <= second).astype(jnp.float32), precision=highest,
        preferred_element_type=jnp.float32,
    )
    total = cumulative[rows - 1 : rows]
    own_total[...] = jnp.broadcast_to(total, own_total.shape)
    tail = jnp.exp(total - cumulative)
    for h in range(heads):
        cut = slice(h * DH, (h + 1) * DH)
        decayed = k_ref[:, cut].astype(jnp.float32) * tail[:, h : h + 1]
        own_state[h] = two_part_dot(decayed, v_ref[:, cut], row_dims).astype(jnp.bfloat16)

    def to_sibling(index):
        pair = ((own_state, sib_state), (own_total, sib_total))[index]
        return remote(*pair, sib_send.at[index], sib_recv.at[index], sibling)

    @pl.when(core == 0)
    def _():
        to_sibling(0).start()
        to_sibling(1).start()

    def chip_copy(r, c, index):
        if index == 0:
            return remote(
                chip_state, got_state.at[chip], st_send.at[r, c], st_recv.at[chip], (sec, 2 * r + c)
            )
        return remote(
            chip_total, got_total.at[chip], tot_send.at[r, c], tot_recv.at[chip], (sec, 2 * r + c)
        )

    @pl.when(core == 1)
    def _():
        to_sibling(0).wait_recv()
        to_sibling(1).wait_recv()
        chip_total[...] = own_total[...] + sib_total[...]
        kept = jnp.exp(total)
        for h in range(heads):
            chip_state[h] = (
                sib_state[h].astype(jnp.float32) * kept[:, h : h + 1]
                + own_state[h].astype(jnp.float32)
            ).astype(jnp.bfloat16)
        for r in range(n_chip - 1, 0, -1):

            @pl.when(chip < r)
            def _():
                for c in range(2):
                    chip_copy(r, c, 1).start()
                    chip_copy(r, c, 0).start()

    for h in range(heads):
        cut = slice(h * DH, (h + 1) * DH)
        spread = cumulative[:, h : h + 1] - turned[h : h + 1, :]
        weights = jnp.exp(jnp.where(causal, spread, -jnp.inf))
        scores = lax.dot_general(
            q_ref[:, cut], k_ref[:, cut], last_dims, preferred_element_type=jnp.float32
        )
        raw[:, cut] = two_part_dot(weights * scores, v_ref[:, cut], plain)

    running[...] = jnp.zeros_like(running)
    for r in range(n_chip - 1):

        @pl.when(r < chip)
        def _():
            remote(
                chip_total, got_total.at[r], tot_send.at[r, 0], tot_recv.at[r], sibling
            ).wait_recv()
            remote(
                chip_state, got_state.at[r], st_send.at[r, 0], st_recv.at[r], sibling
            ).wait_recv()
            kept = jnp.exp(got_total[r][0:1])
            for h in range(heads):
                running[h] = running[h] * kept[:, h : h + 1] + got_state[r, h].astype(jnp.float32)

    @pl.when(core == 1)
    def _():
        kept = jnp.exp(sib_total[0:1])
        for h in range(heads):
            running[h] = running[h] * kept[:, h : h + 1] + sib_state[h].astype(jnp.float32)

    grown = jnp.exp(cumulative)
    for h in range(heads):
        cut = slice(h * DH, (h + 1) * DH)
        state = running[h]
        high = state.astype(jnp.bfloat16)
        low = (state - high.astype(jnp.float32)).astype(jnp.bfloat16)
        carried = jnp.dot(q_ref[:, cut], high, preferred_element_type=jnp.float32) + jnp.dot(
            q_ref[:, cut], low, preferred_element_type=jnp.float32
        )
        whole = raw[:, cut] + grown[:, h : h + 1] * carried
        square = jnp.mean(whole * whole, axis=1, keepdims=True)
        ret[:, cut] = (whole * lax.rsqrt(square + epsilon)).astype(jnp.bfloat16)

    def part_of(s):
        start = pl.multiple_of(s * piece, piece)
        return jnp.dot(ret[...], w_ref[:, pl.ds(start, piece)], preferred_element_type=jnp.float32)

    def part_copy(j):
        return remote(
            send_part.at[j - 1], got_part.at[j - 1], part_send.at[j - 1], part_recv.at[j - 1],
            (lax.rem(sec + j, n_sec), ctx),
        )

    for j in range(1, n_sec):
        send_part[j - 1] = part_of(lax.rem(sec + j, n_sec)).astype(jnp.bfloat16)
        part_copy(j).start()
    summed = part_of(sec)
    for r in range(1, n_ctx):

        @pl.when(r > ctx)
        def _():
            out_ref[r * rows : (r + 1) * rows, :] = jnp.zeros((rows, columns), jnp.bfloat16)

    for j in range(1, n_sec):
        part_copy(j).wait_recv()
        summed += got_part[j - 1].astype(jnp.float32)
    my_rows = pl.ds(pl.multiple_of(ctx * rows, rows), rows)
    my_cut = pl.ds(pl.multiple_of(sec * piece, piece), piece)
    out_ref[my_rows, my_cut] = summed.astype(jnp.bfloat16)

    def z_copy(j):
        spot = out_ref.at[my_rows, my_cut]
        return remote(spot, spot, z_send.at[j - 1], z_recv.at[j - 1], (lax.rem(sec + j, n_sec), ctx))

    def section_at(j):
        return lax.rem(sec + n_sec - j, n_sec)

    def cut_of(s):
        return pl.ds(pl.multiple_of(s * piece, piece), piece)

    def core_of(s):
        return lax.div(s * 2, n_sec)

    def x_copy(r, s):
        spot = out_ref.at[my_rows, cut_of(s)]
        return remote(
            spot, spot, x_send.at[r, s], x_recv.at[ctx, s], (sec, 2 * r + core_of(s))
        )

    def y_copy(d, s):
        spot = out_ref.at[d * rows : (d + 1) * rows, cut_of(s)]
        return remote(spot, spot, y_send.at[d, s], y_recv.at[d, s], sibling)

    def own_copy(s):
        spot = out_ref.at[my_rows, cut_of(s)]
        return remote(spot, spot, y_send.at[n_ctx, s], y_recv.at[n_ctx, s], sibling)

    for j in range(1, n_sec):
        z_copy(j).start()
    for j in range(n_sec):
        s = section_at(j)
        if j:
            z_copy(j).wait_recv()
        for r in range(n_chip - 1, 0, -1):

            @pl.when(r > chip)
            def _():
                x_copy(r, s).start()

        @pl.when(core == 0)
        def _():
            own_copy(s).start()

    for j in range(n_sec):
        s = section_at(j)
        for d in range(n_ctx - 3, -1, -1):

            @pl.when(jnp.logical_and(d < chip * 2, core_of(s) == core))
            def _():
                spot = out_ref.at[d * rows : (d + 1) * rows, cut_of(s)]
                remote(spot, spot, x_send.at[0, 0], x_recv.at[d, s], sibling).wait_recv()
                y_copy(d, s).start()

    for s in range(n_sec):
        for d in range(n_ctx - 2):

            @pl.when(jnp.logical_and(d < chip * 2, core_of(s) != core))
            def _():
                y_copy(d, s).wait_recv()

            @pl.when(jnp.logical_and(d < chip * 2, core_of(s) == core))
            def _():
                y_copy(d, s).wait_send()

    @pl.when(core == 0)
    def _():
        for s in range(n_sec):
            own_copy(s).wait_send()
        to_sibling(0).wait_send()
        to_sibling(1).wait_send()

    @pl.when(core == 1)
    def _():
        for s in range(n_sec):
            spot = out_ref.at[pl.ds(pl.multiple_of((ctx - core) * rows, rows), rows), cut_of(s)]
            remote(spot, spot, y_send.at[n_ctx, s], y_recv.at[n_ctx, s], sibling).wait_recv()

    for r in range(1, n_chip):

        @pl.when(r > chip)
        def _():
            for s in range(n_sec):
                x_copy(r, s).wait_send()

            @pl.when(core == 1)
            def _():
                for c in range(2):
                    chip_copy(r, c, 0).wait_send()
                    chip_copy(r, c, 1).wait_send()

    for j in range(1, n_sec):
        part_copy(j).wait_send()
        z_copy(j).wait_send()


def shared_cache(ret_query, ret_key, ret_value, gate_log, kv_weight):
    n_sec, n_ctx = lax.axis_size("section"), lax.axis_size("ctx")
    n_chip = n_ctx // 2
    rows, width = ret_query.shape
    heads = width // DH
    columns = kv_weight.shape[1]
    piece = columns // n_sec
    gate = jnp.pad(gate_log, ((0, 0), (0, 128 - heads)))
    turned = jnp.pad(gate_log.T, ((0, 8 - heads), (0, 0)))
    state = pltpu.VMEM((heads, DH, DH), jnp.bfloat16)
    total = pltpu.VMEM((8, 128), jnp.float32)
    dma = pltpu.SemaphoreType.DMA
    vmem = pl.BlockSpec(memory_space=pltpu.VMEM)
    return pl.pallas_call(
        functools.partial(cache_kernel, n_sec, n_ctx),
        out_shape=jax.ShapeDtypeStruct((n_ctx * rows, columns), jnp.bfloat16),
        in_specs=[vmem] * 6,
        out_specs=vmem,
        scratch_shapes=[
            pltpu.VMEM((rows, width), jnp.bfloat16),
            pltpu.VMEM((rows, width), jnp.float32),
            state, total, state, total, state, total,
            pltpu.VMEM((n_chip, heads, DH, DH), jnp.bfloat16),
            pltpu.VMEM((n_chip, 8, 128), jnp.float32),
            pltpu.VMEM((heads, DH, DH), jnp.float32),
            pltpu.VMEM((n_sec - 1, rows, piece), jnp.bfloat16),
            pltpu.VMEM((n_sec - 1, rows, piece), jnp.bfloat16),
            dma((2,)), dma((2,)),
            dma((n_chip, 2)), dma((n_chip,)),
            dma((n_chip, 2)), dma((n_chip,)),
            dma((n_sec - 1,)), dma((n_sec - 1,)),
            dma((n_sec - 1,)), dma((n_sec - 1,)),
            dma((n_chip, n_sec)), dma((n_ctx, n_sec)),
            dma((n_ctx + 1, n_sec)), dma((n_ctx + 1, n_sec)),
        ],
        compiler_params=pltpu.CompilerParams(
            collective_id=0, has_side_effects=True, vmem_limit_bytes=LIMIT
        ),
    )(ret_query, ret_key, ret_value, gate, turned, kv_weight)


def attention_kernel(
    n_sec,
    n_ctx,
    q_ref,
    g_ref,
    k_ref,
    v_ref,
    att_ref,
    qg_ref,
    out_ref,
    send_sib,
    keep,
    from_sib,
    got_chip,
    kept,
    send_part,
    got_part,
    final,
    gathered,
    sib_send,
    sib_recv,
    chip_send,
    chip_recv,
    part_send,
    part_recv,
    all_send,
    all_recv,
):
    sec, ctx = lax.axis_index("section"), lax.axis_index("ctx")
    chip, core = lax.div(ctx, 2), lax.rem(ctx, 2)
    n_chip = n_ctx // 2
    sibling = (sec, chip * 2 + 1 - core)
    step = pl.program_id(0)
    kv_heads = kept.shape[0]
    part_heads = kv_heads // n_sec
    layer_count, row_count, width = q_ref.shape
    group = width // DH
    total = k_ref.shape[0]
    pair = 2 * row_count
    scale = 1.0 / math.sqrt(DH)

    others = [
        (lax.rem(sec + j, n_sec), chip * 2 + lax.rem(core + c, 2), j, c)
        for j in range(n_sec)
        for c in range(2)
        if j or c
    ]

    @pl.when(step == 0)
    def _():
        greet(
            [(s, d) for s, d, _, _ in others]
            + [(sec, lax.rem(ctx + 2 * i, n_ctx)) for i in range(1, n_chip)]
        )

    def sib_copy(h):
        return remote(send_sib.at[h], from_sib.at[h], sib_send.at[h], sib_recv.at[h], sibling)

    def chip_copy(r, h):
        return remote(
            keep.at[h, r * pair : (r + 1) * pair, :],
            got_chip.at[chip, h],
            chip_send.at[r, h],
            chip_recv.at[chip, h],
            (sec, 2 * r + core),
        )

    def pass_on(h):
        sib_copy(h).wait_recv()
        mine = pl.ds(pl.multiple_of(chip * pair, pair), pair)
        kept[h] = keep[h, mine, :].astype(jnp.float32) + from_sib[h, mine, :].astype(jnp.float32)
        for r in range(n_chip - 1):

            @pl.when(r < chip)
            def _():
                cut = slice(r * pair, (r + 1) * pair)
                keep[h, cut, :] = (
                    keep[h, cut, :].astype(jnp.float32) + from_sib[h, cut, :].astype(jnp.float32)
                ).astype(jnp.bfloat16)
                chip_copy(r, h).start()

    def place_of(h, c):
        return pl.ds(pl.multiple_of((c * kv_heads + h) * DH, DH), DH)

    def part_copy(h):
        owner = lax.div(h, part_heads)
        return remote(
            send_part.at[h],
            got_part.at[sec, h - owner * part_heads],
            part_send.at[h],
            part_recv.at[sec, h - owner * part_heads],
            (owner, ctx),
        )

    def collect(h):
        for r in range(1, n_chip):

            @pl.when(r > chip)
            def _():
                remote(
                    keep.at[h, 0:pair, :],
                    got_chip.at[r, h],
                    chip_send.at[r, h],
                    chip_recv.at[r, h],
                    sibling,
                ).wait_recv()
                kept[h] += got_chip[r, h].astype(jnp.float32)

        @pl.when(sec != lax.div(h, part_heads))
        def _():
            send_part[h] = kept[h].astype(jnp.bfloat16)
            part_copy(h).start()

    def all_copy(h, s, d, j, c):
        index = h - sec * part_heads
        part = pl.ds(pl.multiple_of(lax.rem(core + c, 2) * row_count, row_count), row_count)
        return remote(
            final.at[index, part, :],
            gathered.at[:, place_of(h, core)],
            all_send.at[index, j, c],
            all_recv.at[h, core],
            (s, d),
        )

    def finish(h):
        @pl.when(sec == lax.div(h, part_heads))
        def _():
            index = h - sec * part_heads
            summed = kept[h]
            for j in range(1, n_sec):
                s = lax.rem(sec + j, n_sec)
                remote(
                    send_part.at[h],
                    got_part.at[s, index],
                    part_send.at[h],
                    part_recv.at[s, index],
                    sibling,
                ).wait_recv()
                summed += got_part[s, index].astype(jnp.float32)
            final[index] = summed.astype(jnp.bfloat16)
            for s, d, j, c in others:
                all_copy(h, s, d, j, c).start()
            own = pl.ds(pl.multiple_of(core * row_count, row_count), row_count)
            gathered[:, place_of(h, core)] = final[index, own, :]

    keys = k_ref[...]
    values = v_ref[...]
    keys_turned = keys.T
    values_turned = values.T
    key_place = lax.broadcasted_iota(jnp.int32, (total, row_count), 0)
    row_place = ctx * row_count + lax.broadcasted_iota(jnp.int32, (total, row_count), 1)
    visible = jnp.concatenate([jnp.where(key_place <= row_place, 0.0, -jnp.inf)] * group, axis=1)

    def stacked(ref, layer):
        return jnp.concatenate(
            [ref[layer, :, j * DH : (j + 1) * DH] for j in range(group)], axis=0
        )

    def spread(ref, layer, rows):
        for j in range(group):
            ref[layer, :, j * DH : (j + 1) * DH] = rows[j * row_count : (j + 1) * row_count]

    key_grad = jnp.zeros((total, DH), jnp.float32)
    value_grad = jnp.zeros((total, DH), jnp.float32)
    for layer in range(layer_count):
        queries = stacked(q_ref, layer)
        grads = stacked(g_ref, layer)
        scores = lax.dot_general(
            keys, queries, (((1,), (1,)), ((), ())), preferred_element_type=jnp.float32
        )
        scores = scores * scale + visible
        top = jnp.max(scores, axis=0, keepdims=True)
        soft = jnp.exp(scores - top)
        soft = soft * (1.0 / jnp.sum(soft, axis=0, keepdims=True))
        low = soft.astype(jnp.bfloat16)
        mixed = jnp.dot(values_turned, low, preferred_element_type=jnp.float32)
        mixed = mixed.T.astype(jnp.bfloat16)
        spread(att_ref, layer, mixed)
        product = grads.astype(jnp.float32) * mixed.astype(jnp.float32)
        delta = jnp.sum(product.T, axis=0, keepdims=True)
        prob_grad = lax.dot_general(
            values, grads, (((1,), (1,)), ((), ())), preferred_element_type=jnp.float32
        )
        score_grad = (soft * (prob_grad - delta) * scale).astype(jnp.bfloat16)
        query_grad = jnp.dot(keys_turned, score_grad, preferred_element_type=jnp.float32)
        spread(qg_ref, layer, query_grad.T.astype(jnp.bfloat16))
        key_grad += jnp.dot(score_grad, queries, preferred_element_type=jnp.float32)
        value_grad += jnp.dot(low, grads, preferred_element_type=jnp.float32)
        if layer == 0:

            @pl.when(step > 0)
            def _():
                pass_on(step - 1)

            @pl.when(step > 1)
            def _():
                collect(step - 2)

            @pl.when(step > 2)
            def _():
                finish(step - 3)

    key_low = key_grad.astype(jnp.bfloat16)
    value_low = value_grad.astype(jnp.bfloat16)

    @pl.when(core == 0)
    def _():
        keep[step] = key_low
        send_sib[step] = value_low

    @pl.when(core == 1)
    def _():
        keep[step] = value_low
        send_sib[step] = key_low

    sib_copy(step).start()

    @pl.when(step == kv_heads - 1)
    def _():
        pass_on(kv_heads - 1)
        for h in range(max(kv_heads - 2, 0), kv_heads):
            collect(h)
        for h in range(max(kv_heads - 3, 0), kv_heads):
            finish(h)
        for h in range(kv_heads):
            for c in range(2):

                @pl.when(jnp.logical_or(sec != h // part_heads, core != c))
                def _():
                    remote(
                        final.at[0, 0:row_count, :],
                        gathered.at[:, place_of(h, c)],
                        all_send.at[0, 0, 0],
                        all_recv.at[h, c],
                        sibling,
                    ).wait_recv()

        out_ref[...] = gathered[...]
        for h in range(kv_heads):
            sib_copy(h).wait_send()
            for r in range(n_chip - 1):

                @pl.when(r < chip)
                def _():
                    chip_copy(r, h).wait_send()

            @pl.when(sec != h // part_heads)
            def _():
                part_copy(h).wait_send()

            @pl.when(sec == h // part_heads)
            def _():
                for s, d, j, c in others:
                    all_copy(h, s, d, j, c).wait_send()


def cross_attention(queries, cotangent, full_cache):
    n_sec, n_ctx = lax.axis_size("section"), lax.axis_size("ctx")
    n_chip = n_ctx // 2
    layer_count, row_count, model_width = queries.shape
    total, cache_width = full_cache.shape
    kv_heads = cache_width // 2 // DH
    width = model_width // kv_heads
    pair = 2 * row_count
    part_heads = kv_heads // n_sec
    rows = pl.BlockSpec((layer_count, row_count, width), lambda h: (0, 0, h))
    cut = pl.BlockSpec((total, DH), lambda h: (0, h))
    cut_values = pl.BlockSpec((total, DH), lambda h: (0, kv_heads + h))
    dma = pltpu.SemaphoreType.DMA
    per_head = pltpu.VMEM((kv_heads, total, DH), jnp.bfloat16)
    return pl.pallas_call(
        functools.partial(attention_kernel, n_sec, n_ctx),
        grid=(kv_heads,),
        in_specs=[rows, rows, cut, cut_values],
        out_specs=[rows, rows, pl.BlockSpec((row_count, cache_width), lambda h: (0, 0))],
        out_shape=[
            jax.ShapeDtypeStruct(queries.shape, jnp.bfloat16),
            jax.ShapeDtypeStruct(queries.shape, jnp.bfloat16),
            jax.ShapeDtypeStruct((row_count, cache_width), jnp.bfloat16),
        ],
        scratch_shapes=[
            per_head, per_head, per_head,
            pltpu.VMEM((n_chip, kv_heads, pair, DH), jnp.bfloat16),
            pltpu.VMEM((kv_heads, pair, DH), jnp.float32),
            pltpu.VMEM((kv_heads, pair, DH), jnp.bfloat16),
            pltpu.VMEM((n_sec, part_heads, pair, DH), jnp.bfloat16),
            pltpu.VMEM((part_heads, pair, DH), jnp.bfloat16),
            pltpu.VMEM((row_count, cache_width), jnp.bfloat16),
            dma((kv_heads,)), dma((kv_heads,)),
            dma((n_chip, kv_heads)), dma((n_chip, kv_heads)),
            dma((kv_heads,)), dma((n_sec, part_heads)),
            dma((part_heads, n_sec, 2)), dma((kv_heads, 2)),
        ],
        compiler_params=pltpu.CompilerParams(
            collective_id=1, has_side_effects=True, vmem_limit_bytes=LIMIT
        ),
    )(queries, cotangent, full_cache, full_cache)


def body(queries, cotangent, ret_query, ret_key, ret_value, gate_log, kv_weight):
    full_cache = shared_cache(ret_query, ret_key, ret_value, gate_log, kv_weight)
    attended_all, grad_rows_all, cache_grad = cross_attention(queries, cotangent, full_cache)
    retention_grad = jnp.einsum(
        "rw,cw->rc", cache_grad, kv_weight, preferred_element_type=jnp.float32
    ).astype(jnp.bfloat16)
    return (attended_all, grad_rows_all, retention_grad)


def solution(mesh):
    return jax.shard_map(
        body,
        mesh=mesh,
        in_specs=(
            P("section", "ctx", None),
            P("section", "ctx", None),
            P("ctx", "section"),
            P("ctx", "section"),
            P("ctx", "section"),
            P("ctx", "section"),
            P("section", None),
        ),
        out_specs=(P("section", "ctx", None), P("section", "ctx", None), P("ctx", "section")),
        check_vma=False,
    )
```

```python
import functools
import math

import jax
import jax.numpy as jnp
from jax import lax
from jax.experimental import pallas as pl
from jax.experimental.pallas import tpu as pltpu
from jax.sharding import PartitionSpec as P

DH = 128


epsilon = 1e-06
highest = lax.Precision.HIGHEST

MESH = pl.DeviceIdType.MESH
LIMIT = 56 * 1024 * 1024


def greet(peers):
    barrier = pltpu.get_barrier_semaphore()
    for peer in peers:
        pl.semaphore_signal(barrier, inc=1, device_id=peer, device_id_type=MESH)
    pl.semaphore_wait(barrier, len(peers))


def remote(source, target, send_sem, recv_sem, device):
    return pltpu.make_async_remote_copy(
        src_ref=source,
        dst_ref=target,
        send_sem=send_sem,
        recv_sem=recv_sem,
        device_id=device,
        device_id_type=MESH,
    )


def two_part_dot(wide, narrow, dims):
    high = wide.astype(jnp.bfloat16)
    low = (wide - high.astype(jnp.float32)).astype(jnp.bfloat16)
    return lax.dot_general(
        high, narrow, dims, preferred_element_type=jnp.float32
    ) + lax.dot_general(low, narrow, dims, preferred_element_type=jnp.float32)


def cache_kernel(
    n_sec,
    n_ctx,
    q_ref,
    k_ref,
    v_ref,
    gate_ref,
    turned_ref,
    w_ref,
    out_ref,
    ret,
    raw,
    own_state,
    own_total,
    sib_state,
    sib_total,
    chip_state,
    chip_total,
    got_state,
    got_total,
    running,
    send_part,
    got_part,
    sib_send,
    sib_recv,
    st_send,
    st_recv,
    tot_send,
    tot_recv,
    part_send,
    part_recv,
    z_send,
    z_recv,
):
    sec, ctx = lax.axis_index("section"), lax.axis_index("ctx")
    chip, core = lax.div(ctx, 2), lax.rem(ctx, 2)
    n_chip = n_ctx // 2
    sibling = (sec, chip * 2 + 1 - core)
    rows, width = q_ref.shape
    heads = width // DH
    columns = out_ref.shape[1]
    piece = columns // n_sec
    row_dims = (((0,), (0,)), ((), ()))
    plain = (((1,), (0,)), ((), ()))
    last_dims = (((1,), (1,)), ((), ()))

    greet(
        [(lax.rem(sec + j, n_sec), ctx) for j in range(1, n_sec)]
        + [(sec, lax.rem(ctx + j, n_ctx)) for j in range(1, n_ctx)]
    )

    first = lax.broadcasted_iota(jnp.int32, (rows, rows), 0)
    second = lax.broadcasted_iota(jnp.int32, (rows, rows), 1)
    causal = first >= second
    cumulative = jnp.dot(
        causal.astype(jnp.float32), gate_ref[...], precision=highest,
        preferred_element_type=jnp.float32,
    )
    turned = jnp.dot(
        turned_ref[...], (first <= second).astype(jnp.float32), precision=highest,
        preferred_element_type=jnp.float32,
    )
    total = cumulative[rows - 1 : rows]
    own_total[...] = jnp.broadcast_to(total, own_total.shape)
    tail = jnp.exp(total - cumulative)
    for h in range(heads):
        cut = slice(h * DH, (h + 1) * DH)
        decayed = k_ref[:, cut].astype(jnp.float32) * tail[:, h : h + 1]
        own_state[h] = two_part_dot(decayed, v_ref[:, cut], row_dims).astype(jnp.bfloat16)

    def to_sibling(index):
        pair = ((own_state, sib_state), (own_total, sib_total))[index]
        return remote(*pair, sib_send.at[index], sib_recv.at[index], sibling)

    @pl.when(core == 0)
    def _():
        to_sibling(0).start()
        to_sibling(1).start()

    def chip_copy(r, c, index):
        if index == 0:
            return remote(
                chip_state, got_state.at[chip], st_send.at[r, c], st_recv.at[chip], (sec, 2 * r + c)
            )
        return remote(
            chip_total, got_total.at[chip], tot_send.at[r, c], tot_recv.at[chip], (sec, 2 * r + c)
        )

    @pl.when(core == 1)
    def _():
        to_sibling(0).wait_recv()
        to_sibling(1).wait_recv()
        chip_total[...] = own_total[...] + sib_total[...]
        kept = jnp.exp(total)
        for h in range(heads):
            chip_state[h] = (
                sib_state[h].astype(jnp.float32) * kept[:, h : h + 1]
                + own_state[h].astype(jnp.float32)
            ).astype(jnp.bfloat16)
        for r in range(n_chip - 1, 0, -1):

            @pl.when(chip < r)
            def _():
                for c in range(2):
                    chip_copy(r, c, 1).start()
                    chip_copy(r, c, 0).start()

    for h in range(heads):
        cut = slice(h * DH, (h + 1) * DH)
        spread = cumulative[:, h : h + 1] - turned[h : h + 1, :]
        weights = jnp.exp(jnp.where(causal, spread, -jnp.inf))
        scores = lax.dot_general(
            q_ref[:, cut], k_ref[:, cut], last_dims, preferred_element_type=jnp.float32
        )
        raw[:, cut] = two_part_dot(weights * scores, v_ref[:, cut], plain)

    running[...] = jnp.zeros_like(running)
    for r in range(n_chip - 1):

        @pl.when(r < chip)
        def _():
            remote(
                chip_total, got_total.at[r], tot_send.at[r, 0], tot_recv.at[r], sibling
            ).wait_recv()
            remote(
                chip_state, got_state.at[r], st_send.at[r, 0], st_recv.at[r], sibling
            ).wait_recv()
            kept = jnp.exp(got_total[r][0:1])
            for h in range(heads):
                running[h] = running[h] * kept[:, h : h + 1] + got_state[r, h].astype(jnp.float32)

    @pl.when(core == 1)
    def _():
        kept = jnp.exp(sib_total[0:1])
        for h in range(heads):
            running[h] = running[h] * kept[:, h : h + 1] + sib_state[h].astype(jnp.float32)

    grown = jnp.exp(cumulative)
    for h in range(heads):
        cut = slice(h * DH, (h + 1) * DH)
        state = running[h]
        high = state.astype(jnp.bfloat16)
        low = (state - high.astype(jnp.float32)).astype(jnp.bfloat16)
        carried = jnp.dot(q_ref[:, cut], high, preferred_element_type=jnp.float32) + jnp.dot(
            q_ref[:, cut], low, preferred_element_type=jnp.float32
        )
        whole = raw[:, cut] + grown[:, h : h + 1] * carried
        square = jnp.mean(whole * whole, axis=1, keepdims=True)
        ret[:, cut] = (whole * lax.rsqrt(square + epsilon)).astype(jnp.bfloat16)

    def part_of(s):
        start = pl.multiple_of(s * piece, piece)
        return jnp.dot(ret[...], w_ref[:, pl.ds(start, piece)], preferred_element_type=jnp.float32)

    def part_copy(j):
        return remote(
            send_part.at[j - 1], got_part.at[j - 1], part_send.at[j - 1], part_recv.at[j - 1],
            (lax.rem(sec + j, n_sec), ctx),
        )

    for j in range(1, n_sec):
        send_part[j - 1] = part_of(lax.rem(sec + j, n_sec)).astype(jnp.bfloat16)
        part_copy(j).start()
    summed = part_of(sec)
    for j in range(1, n_sec):
        part_copy(j).wait_recv()
        summed += got_part[j - 1].astype(jnp.float32)
    my_cut = pl.ds(pl.multiple_of(sec * piece, piece), piece)
    out_ref[:, my_cut] = summed.astype(jnp.bfloat16)

    def z_copy(j):
        spot = out_ref.at[:, my_cut]
        return remote(spot, spot, z_send.at[j - 1], z_recv.at[j - 1], (lax.rem(sec + j, n_sec), ctx))

    for j in range(1, n_sec):
        z_copy(j).start()
    for j in range(1, n_sec):
        z_copy(j).wait_recv()

    @pl.when(core == 0)
    def _():
        to_sibling(0).wait_send()
        to_sibling(1).wait_send()

    for r in range(1, n_chip):

        @pl.when(r > chip)
        def _():
            @pl.when(core == 1)
            def _():
                for c in range(2):
                    chip_copy(r, c, 0).wait_send()
                    chip_copy(r, c, 1).wait_send()

    for j in range(1, n_sec):
        part_copy(j).wait_send()
        z_copy(j).wait_send()


def shared_cache(ret_query, ret_key, ret_value, gate_log, kv_weight):
    n_sec, n_ctx = lax.axis_size("section"), lax.axis_size("ctx")
    n_chip = n_ctx // 2
    rows, width = ret_query.shape
    heads = width // DH
    columns = kv_weight.shape[1]
    piece = columns // n_sec
    gate = jnp.pad(gate_log, ((0, 0), (0, 128 - heads)))
    turned = jnp.pad(gate_log.T, ((0, 8 - heads), (0, 0)))
    state = pltpu.VMEM((heads, DH, DH), jnp.bfloat16)
    total = pltpu.VMEM((8, 128), jnp.float32)
    dma = pltpu.SemaphoreType.DMA
    vmem = pl.BlockSpec(memory_space=pltpu.VMEM)
    return pl.pallas_call(
        functools.partial(cache_kernel, n_sec, n_ctx),
        out_shape=jax.ShapeDtypeStruct((rows, columns), jnp.bfloat16),
        in_specs=[vmem] * 6,
        out_specs=vmem,
        scratch_shapes=[
            pltpu.VMEM((rows, width), jnp.bfloat16),
            pltpu.VMEM((rows, width), jnp.float32),
            state, total, state, total, state, total,
            pltpu.VMEM((n_chip, heads, DH, DH), jnp.bfloat16),
            pltpu.VMEM((n_chip, 8, 128), jnp.float32),
            pltpu.VMEM((heads, DH, DH), jnp.float32),
            pltpu.VMEM((n_sec - 1, rows, piece), jnp.bfloat16),
            pltpu.VMEM((n_sec - 1, rows, piece), jnp.bfloat16),
            dma((2,)), dma((2,)),
            dma((n_chip, 2)), dma((n_chip,)),
            dma((n_chip, 2)), dma((n_chip,)),
            dma((n_sec - 1,)), dma((n_sec - 1,)),
            dma((n_sec - 1,)), dma((n_sec - 1,)),
        ],
        compiler_params=pltpu.CompilerParams(
            collective_id=0, has_side_effects=True, vmem_limit_bytes=LIMIT
        ),
    )(ret_query, ret_key, ret_value, gate, turned, kv_weight)


def attention_kernel(
    n_sec,
    n_ctx,
    q_ref,
    g_ref,
    block_ref,
    att_ref,
    qg_ref,
    out_ref,
    send_sib,
    keep,
    from_sib,
    got_chip,
    kept,
    send_part,
    got_part,
    final,
    gathered,
    cache,
    sib_send,
    sib_recv,
    chip_send,
    chip_recv,
    part_send,
    part_recv,
    all_send,
    all_recv,
    x_send,
    x_recv,
    y_send,
    y_recv,
):
    sec, ctx = lax.axis_index("section"), lax.axis_index("ctx")
    chip, core = lax.div(ctx, 2), lax.rem(ctx, 2)
    n_chip = n_ctx // 2
    sibling = (sec, chip * 2 + 1 - core)
    step = pl.program_id(0)
    kv_heads = kept.shape[0]
    part_heads = kv_heads // n_sec
    layer_count, row_count, width = q_ref.shape
    group = width // DH
    total = n_ctx * row_count
    pair = 2 * row_count
    scale = 1.0 / math.sqrt(DH)

    others = [
        (lax.rem(sec + j, n_sec), chip * 2 + lax.rem(core + c, 2), j, c)
        for j in range(n_sec)
        for c in range(2)
        if j or c
    ]

    my_rows = pl.ds(pl.multiple_of(ctx * row_count, row_count), row_count)

    def rows_of(d):
        return pl.ds(d * row_count, row_count)

    def x_copy(r, h, c):
        spot = cache.at[c, h, my_rows, :]
        return remote(spot, spot, x_send.at[r, h, c], x_recv.at[ctx, h], (sec, 2 * r + c))

    def y_copy(d, h):
        spot = cache.at[core, h, rows_of(d), :]
        return remote(spot, spot, y_send.at[d, h], y_recv.at[d, h], sibling)

    def own_copy(h, c):
        spot = cache.at[c, h, my_rows, :]
        return remote(spot, spot, y_send.at[n_ctx + c, h], y_recv.at[n_ctx + c, h], sibling)

    def forward(h):
        for d in range(n_ctx - 2):

            @pl.when(d < chip * 2)
            def _():
                spot = cache.at[core, h, rows_of(d), :]
                remote(spot, spot, x_send.at[0, h, 0], x_recv.at[d, h], sibling).wait_recv()
                y_copy(d, h).start()

    def arrive(h):
        for d in range(n_ctx - 2):

            @pl.when(d < chip * 2)
            def _():
                spot = cache.at[1 - core, h, rows_of(d), :]
                remote(spot, spot, y_send.at[d, h], y_recv.at[d, h], sibling).wait_recv()

        @pl.when(core == 1)
        def _():
            before = pl.ds(pl.multiple_of(chip * 2 * row_count, row_count), row_count)
            for c in range(2):
                spot = cache.at[c, h, before, :]
                remote(
                    spot, spot, y_send.at[n_ctx + c, h], y_recv.at[n_ctx + c, h], sibling
                ).wait_recv()

    @pl.when(step == 0)
    def _():
        for h in range(kv_heads):
            for c in range(2):
                at = (c * kv_heads + h) * DH
                cache[c, h, my_rows, :] = block_ref[:, at : at + DH]
        greet(
            [(s, d) for s, d, _, _ in others]
            + [
                (sec, lax.rem(chip + i, n_chip) * 2 + c)
                for i in range(1, n_chip)
                for c in range(2)
            ]
        )
        for h in range(kv_heads):
            for r in range(n_chip - 1, 0, -1):

                @pl.when(r > chip)
                def _():
                    for c in range(2):
                        x_copy(r, h, c).start()

            @pl.when(core == 0)
            def _():
                for c in range(2):
                    own_copy(h, c).start()

        for d in range(1, n_ctx):

            @pl.when(d > ctx)
            def _():
                for c in range(2):
                    for h in range(kv_heads):
                        cache[c, h, d * row_count : (d + 1) * row_count, :] = jnp.zeros(
                            (row_count, DH), jnp.bfloat16
                        )

        forward(0)

    arrive(step)

    def sib_copy(h):
        return remote(send_sib.at[h], from_sib.at[h], sib_send.at[h], sib_recv.at[h], sibling)

    def chip_copy(r, h):
        return remote(
            keep.at[h, r * pair : (r + 1) * pair, :],
            got_chip.at[chip, h],
            chip_send.at[r, h],
            chip_recv.at[chip, h],
            (sec, 2 * r + core),
        )

    def pass_on(h):
        sib_copy(h).wait_recv()
        mine = pl.ds(pl.multiple_of(chip * pair, pair), pair)
        kept[h] = keep[h, mine, :].astype(jnp.float32) + from_sib[h, mine, :].astype(jnp.float32)
        for r in range(n_chip - 1):

            @pl.when(r < chip)
            def _():
                cut = slice(r * pair, (r + 1) * pair)
                keep[h, cut, :] = (
                    keep[h, cut, :].astype(jnp.float32) + from_sib[h, cut, :].astype(jnp.float32)
                ).astype(jnp.bfloat16)
                chip_copy(r, h).start()

    def place_of(h, c):
        return pl.ds(pl.multiple_of((c * kv_heads + h) * DH, DH), DH)

    def part_copy(h):
        owner = lax.div(h, part_heads)
        return remote(
            send_part.at[h],
            got_part.at[sec, h - owner * part_heads],
            part_send.at[h],
            part_recv.at[sec, h - owner * part_heads],
            (owner, ctx),
        )

    def collect(h):
        for r in range(1, n_chip):

            @pl.when(r > chip)
            def _():
                remote(
                    keep.at[h, 0:pair, :],
                    got_chip.at[r, h],
                    chip_send.at[r, h],
                    chip_recv.at[r, h],
                    sibling,
                ).wait_recv()
                kept[h] += got_chip[r, h].astype(jnp.float32)

        @pl.when(sec != lax.div(h, part_heads))
        def _():
            send_part[h] = kept[h].astype(jnp.bfloat16)
            part_copy(h).start()

    def all_copy(h, s, d, j, c):
        index = h - sec * part_heads
        part = pl.ds(pl.multiple_of(lax.rem(core + c, 2) * row_count, row_count), row_count)
        return remote(
            final.at[index, part, :],
            gathered.at[:, place_of(h, core)],
            all_send.at[index, j, c],
            all_recv.at[h, core],
            (s, d),
        )

    def finish(h):
        @pl.when(sec == lax.div(h, part_heads))
        def _():
            index = h - sec * part_heads
            summed = kept[h]
            for j in range(1, n_sec):
                s = lax.rem(sec + j, n_sec)
                remote(
                    send_part.at[h],
                    got_part.at[s, index],
                    part_send.at[h],
                    part_recv.at[s, index],
                    sibling,
                ).wait_recv()
                summed += got_part[s, index].astype(jnp.float32)
            final[index] = summed.astype(jnp.bfloat16)
            for s, d, j, c in others:
                all_copy(h, s, d, j, c).start()
            own = pl.ds(pl.multiple_of(core * row_count, row_count), row_count)
            gathered[:, place_of(h, core)] = final[index, own, :]

    keys = cache[0, step]
    values = cache[1, step]
    keys_turned = keys.T
    values_turned = values.T
    key_place = lax.broadcasted_iota(jnp.int32, (total, row_count), 0)
    row_place = ctx * row_count + lax.broadcasted_iota(jnp.int32, (total, row_count), 1)
    visible = jnp.concatenate([jnp.where(key_place <= row_place, 0.0, -jnp.inf)] * group, axis=1)

    def stacked(ref, layer):
        return jnp.concatenate(
            [ref[layer, :, j * DH : (j + 1) * DH] for j in range(group)], axis=0
        )

    def spread(ref, layer, rows):
        for j in range(group):
            ref[layer, :, j * DH : (j + 1) * DH] = rows[j * row_count : (j + 1) * row_count]

    key_grad = jnp.zeros((total, DH), jnp.float32)
    value_grad = jnp.zeros((total, DH), jnp.float32)
    for layer in range(layer_count):
        queries = stacked(q_ref, layer)
        grads = stacked(g_ref, layer)
        scores = lax.dot_general(
            keys, queries, (((1,), (1,)), ((), ())), preferred_element_type=jnp.float32
        )
        scores = scores * scale + visible
        top = jnp.max(scores, axis=0, keepdims=True)
        soft = jnp.exp(scores - top)
        soft = soft * (1.0 / jnp.sum(soft, axis=0, keepdims=True))
        low = soft.astype(jnp.bfloat16)
        mixed = jnp.dot(values_turned, low, preferred_element_type=jnp.float32)
        mixed = mixed.T.astype(jnp.bfloat16)
        spread(att_ref, layer, mixed)
        product = grads.astype(jnp.float32) * mixed.astype(jnp.float32)
        delta = jnp.sum(product.T, axis=0, keepdims=True)
        prob_grad = lax.dot_general(
            values, grads, (((1,), (1,)), ((), ())), preferred_element_type=jnp.float32
        )
        score_grad = (soft * (prob_grad - delta) * scale).astype(jnp.bfloat16)
        query_grad = jnp.dot(keys_turned, score_grad, preferred_element_type=jnp.float32)
        spread(qg_ref, layer, query_grad.T.astype(jnp.bfloat16))
        key_grad += jnp.dot(score_grad, queries, preferred_element_type=jnp.float32)
        value_grad += jnp.dot(low, grads, preferred_element_type=jnp.float32)
        if layer == 0:

            @pl.when(step < kv_heads - 1)
            def _():
                forward(step + 1)

            @pl.when(step > 0)
            def _():
                pass_on(step - 1)

            @pl.when(step > 1)
            def _():
                collect(step - 2)

            @pl.when(step > 2)
            def _():
                finish(step - 3)

    key_low = key_grad.astype(jnp.bfloat16)
    value_low = value_grad.astype(jnp.bfloat16)

    @pl.when(core == 0)
    def _():
        keep[step] = key_low
        send_sib[step] = value_low

    @pl.when(core == 1)
    def _():
        keep[step] = value_low
        send_sib[step] = key_low

    sib_copy(step).start()

    @pl.when(step == kv_heads - 1)
    def _():
        pass_on(kv_heads - 1)
        for h in range(max(kv_heads - 2, 0), kv_heads):
            collect(h)
        for h in range(max(kv_heads - 3, 0), kv_heads):
            finish(h)
        for h in range(kv_heads):
            for c in range(2):

                @pl.when(jnp.logical_or(sec != h // part_heads, core != c))
                def _():
                    remote(
                        final.at[0, 0:row_count, :],
                        gathered.at[:, place_of(h, c)],
                        all_send.at[0, 0, 0],
                        all_recv.at[h, c],
                        sibling,
                    ).wait_recv()

        out_ref[...] = gathered[...]
        for h in range(kv_heads):
            sib_copy(h).wait_send()
            for r in range(1, n_chip):

                @pl.when(r > chip)
                def _():
                    for c in range(2):
                        x_copy(r, h, c).wait_send()

            for d in range(n_ctx - 2):

                @pl.when(d < chip * 2)
                def _():
                    y_copy(d, h).wait_send()

            @pl.when(core == 0)
            def _():
                for c in range(2):
                    own_copy(h, c).wait_send()

            for r in range(n_chip - 1):

                @pl.when(r < chip)
                def _():
                    chip_copy(r, h).wait_send()

            @pl.when(sec != h // part_heads)
            def _():
                part_copy(h).wait_send()

            @pl.when(sec == h // part_heads)
            def _():
                for s, d, j, c in others:
                    all_copy(h, s, d, j, c).wait_send()


def cross_attention(queries, cotangent, block):
    n_sec, n_ctx = lax.axis_size("section"), lax.axis_size("ctx")
    n_chip = n_ctx // 2
    layer_count, row_count, model_width = queries.shape
    cache_width = block.shape[1]
    total = n_ctx * row_count
    kv_heads = cache_width // 2 // DH
    width = model_width // kv_heads
    pair = 2 * row_count
    part_heads = kv_heads // n_sec
    rows = pl.BlockSpec((layer_count, row_count, width), lambda h: (0, 0, h))
    whole = pl.BlockSpec((row_count, cache_width), lambda h: (0, 0))
    dma = pltpu.SemaphoreType.DMA
    per_head = pltpu.VMEM((kv_heads, total, DH), jnp.bfloat16)
    return pl.pallas_call(
        functools.partial(attention_kernel, n_sec, n_ctx),
        grid=(kv_heads,),
        in_specs=[rows, rows, whole],
        out_specs=[rows, rows, whole],
        out_shape=[
            jax.ShapeDtypeStruct(queries.shape, jnp.bfloat16),
            jax.ShapeDtypeStruct(queries.shape, jnp.bfloat16),
            jax.ShapeDtypeStruct((row_count, cache_width), jnp.bfloat16),
        ],
        scratch_shapes=[
            per_head, per_head, per_head,
            pltpu.VMEM((n_chip, kv_heads, pair, DH), jnp.bfloat16),
            pltpu.VMEM((kv_heads, pair, DH), jnp.float32),
            pltpu.VMEM((kv_heads, pair, DH), jnp.bfloat16),
            pltpu.VMEM((n_sec, part_heads, pair, DH), jnp.bfloat16),
            pltpu.VMEM((part_heads, pair, DH), jnp.bfloat16),
            pltpu.VMEM((row_count, cache_width), jnp.bfloat16),
            pltpu.VMEM((2, kv_heads, total, DH), jnp.bfloat16),
            dma((kv_heads,)), dma((kv_heads,)),
            dma((n_chip, kv_heads)), dma((n_chip, kv_heads)),
            dma((kv_heads,)), dma((n_sec, part_heads)),
            dma((part_heads, n_sec, 2)), dma((kv_heads, 2)),
            dma((n_chip, kv_heads, 2)), dma((n_ctx, kv_heads)),
            dma((n_ctx + 2, kv_heads)), dma((n_ctx + 2, kv_heads)),
        ],
        compiler_params=pltpu.CompilerParams(
            collective_id=1, has_side_effects=True, vmem_limit_bytes=LIMIT
        ),
    )(queries, cotangent, block)


def body(queries, cotangent, ret_query, ret_key, ret_value, gate_log, kv_weight):
    block = shared_cache(ret_query, ret_key, ret_value, gate_log, kv_weight)
    attended_all, grad_rows_all, cache_grad = cross_attention(queries, cotangent, block)
    retention_grad = jnp.einsum(
        "rw,cw->rc", cache_grad, kv_weight, preferred_element_type=jnp.float32
    ).astype(jnp.bfloat16)
    return (attended_all, grad_rows_all, retention_grad)


def solution(mesh):
    return jax.shard_map(
        body,
        mesh=mesh,
        in_specs=(
            P("section", "ctx", None),
            P("section", "ctx", None),
            P("ctx", "section"),
            P("ctx", "section"),
            P("ctx", "section"),
            P("ctx", "section"),
            P("section", None),
        ),
        out_specs=(P("section", "ctx", None), P("section", "ctx", None), P("ctx", "section")),
        check_vma=False,
    )
```

```python
import functools
import math

import jax
import jax.numpy as jnp
from jax import lax
from jax.experimental import pallas as pl
from jax.experimental.pallas import tpu as pltpu
from jax.sharding import PartitionSpec as P

DH = 128


epsilon = 1e-06
highest = lax.Precision.HIGHEST

MESH = pl.DeviceIdType.MESH
LIMIT = 56 * 1024 * 1024


def greet(peers):
    barrier = pltpu.get_barrier_semaphore()
    for peer in peers:
        pl.semaphore_signal(barrier, inc=1, device_id=peer, device_id_type=MESH)
    pl.semaphore_wait(barrier, len(peers))


def remote(source, target, send_sem, recv_sem, device):
    return pltpu.make_async_remote_copy(
        src_ref=source,
        dst_ref=target,
        send_sem=send_sem,
        recv_sem=recv_sem,
        device_id=device,
        device_id_type=MESH,
    )


def two_part_dot(wide, narrow, dims):
    high = wide.astype(jnp.bfloat16)
    low = (wide - high.astype(jnp.float32)).astype(jnp.bfloat16)
    return lax.dot_general(
        high, narrow, dims, preferred_element_type=jnp.float32
    ) + lax.dot_general(low, narrow, dims, preferred_element_type=jnp.float32)


def cache_kernel(
    n_sec,
    n_ctx,
    q_ref,
    k_ref,
    v_ref,
    gate_ref,
    turned_ref,
    w_ref,
    out_ref,
    ret,
    raw,
    own_state,
    own_total,
    sib_state,
    sib_total,
    chip_state,
    chip_total,
    got_state,
    got_total,
    running,
    send_part,
    got_part,
    sib_send,
    sib_recv,
    st_send,
    st_recv,
    tot_send,
    tot_recv,
    part_send,
    part_recv,
    z_send,
    z_recv,
):
    sec, ctx = lax.axis_index("section"), lax.axis_index("ctx")
    chip, core = lax.div(ctx, 2), lax.rem(ctx, 2)
    n_chip = n_ctx // 2
    sibling = (sec, chip * 2 + 1 - core)
    rows, width = q_ref.shape
    heads = width // DH
    columns = out_ref.shape[1]
    piece = columns // n_sec
    row_dims = (((0,), (0,)), ((), ()))
    plain = (((1,), (0,)), ((), ()))
    last_dims = (((1,), (1,)), ((), ()))

    greet(
        [(lax.rem(sec + j, n_sec), ctx) for j in range(1, n_sec)]
        + [(sec, lax.rem(ctx + j, n_ctx)) for j in range(1, n_ctx)]
    )

    first = lax.broadcasted_iota(jnp.int32, (rows, rows), 0)
    second = lax.broadcasted_iota(jnp.int32, (rows, rows), 1)
    causal = first >= second
    cumulative = jnp.dot(
        causal.astype(jnp.float32), gate_ref[...], precision=highest,
        preferred_element_type=jnp.float32,
    )
    turned = jnp.dot(
        turned_ref[...], (first <= second).astype(jnp.float32), precision=highest,
        preferred_element_type=jnp.float32,
    )
    total = cumulative[rows - 1 : rows]
    own_total[...] = jnp.broadcast_to(total, own_total.shape)
    tail = jnp.exp(total - cumulative)
    for h in range(heads):
        cut = slice(h * DH, (h + 1) * DH)
        decayed = k_ref[:, cut].astype(jnp.float32) * tail[:, h : h + 1]
        own_state[h] = two_part_dot(decayed, v_ref[:, cut], row_dims).astype(jnp.bfloat16)

    def to_sibling(index):
        pair = ((own_state, sib_state), (own_total, sib_total))[index]
        return remote(*pair, sib_send.at[index], sib_recv.at[index], sibling)

    @pl.when(core == 0)
    def _():
        to_sibling(0).start()
        to_sibling(1).start()

    def chip_copy(r, c, index):
        if index == 0:
            return remote(
                chip_state, got_state.at[chip], st_send.at[r, c], st_recv.at[chip], (sec, 2 * r + c)
            )
        return remote(
            chip_total, got_total.at[chip], tot_send.at[r, c], tot_recv.at[chip], (sec, 2 * r + c)
        )

    @pl.when(core == 1)
    def _():
        to_sibling(0).wait_recv()
        to_sibling(1).wait_recv()
        chip_total[...] = own_total[...] + sib_total[...]
        kept = jnp.exp(total)
        for h in range(heads):
            chip_state[h] = (
                sib_state[h].astype(jnp.float32) * kept[:, h : h + 1]
                + own_state[h].astype(jnp.float32)
            ).astype(jnp.bfloat16)
        for r in range(n_chip - 1, 0, -1):

            @pl.when(chip < r)
            def _():
                for c in range(2):
                    chip_copy(r, c, 1).start()
                    chip_copy(r, c, 0).start()

    for h in range(heads):
        cut = slice(h * DH, (h + 1) * DH)
        spread = cumulative[:, h : h + 1] - turned[h : h + 1, :]
        weights = jnp.exp(jnp.where(causal, spread, -jnp.inf))
        scores = lax.dot_general(
            q_ref[:, cut], k_ref[:, cut], last_dims, preferred_element_type=jnp.float32
        )
        raw[:, cut] = two_part_dot(weights * scores, v_ref[:, cut], plain)

    running[...] = jnp.zeros_like(running)
    for r in range(n_chip - 1):

        @pl.when(r < chip)
        def _():
            remote(
                chip_total, got_total.at[r], tot_send.at[r, 0], tot_recv.at[r], sibling
            ).wait_recv()
            remote(
                chip_state, got_state.at[r], st_send.at[r, 0], st_recv.at[r], sibling
            ).wait_recv()
            kept = jnp.exp(got_total[r][0:1])
            for h in range(heads):
                running[h] = running[h] * kept[:, h : h + 1] + got_state[r, h].astype(jnp.float32)

    @pl.when(core == 1)
    def _():
        kept = jnp.exp(sib_total[0:1])
        for h in range(heads):
            running[h] = running[h] * kept[:, h : h + 1] + sib_state[h].astype(jnp.float32)

    grown = jnp.exp(cumulative)
    for h in range(heads):
        cut = slice(h * DH, (h + 1) * DH)
        state = running[h]
        high = state.astype(jnp.bfloat16)
        low = (state - high.astype(jnp.float32)).astype(jnp.bfloat16)
        carried = jnp.dot(q_ref[:, cut], high, preferred_element_type=jnp.float32) + jnp.dot(
            q_ref[:, cut], low, preferred_element_type=jnp.float32
        )
        whole = raw[:, cut] + grown[:, h : h + 1] * carried
        square = jnp.mean(whole * whole, axis=1, keepdims=True)
        ret[:, cut] = (whole * lax.rsqrt(square + epsilon)).astype(jnp.bfloat16)

    def part_of(s):
        start = pl.multiple_of(s * piece, piece)
        return jnp.dot(ret[...], w_ref[:, pl.ds(start, piece)], preferred_element_type=jnp.float32)

    def part_copy(j):
        return remote(
            send_part.at[j - 1], got_part.at[j - 1], part_send.at[j - 1], part_recv.at[j - 1],
            (lax.rem(sec + j, n_sec), ctx),
        )

    for j in range(1, n_sec):
        send_part[j - 1] = part_of(lax.rem(sec + j, n_sec)).astype(jnp.bfloat16)
        part_copy(j).start()
    summed = part_of(sec)
    for j in range(1, n_sec):
        part_copy(j).wait_recv()
        summed += got_part[j - 1].astype(jnp.float32)
    my_cut = pl.ds(pl.multiple_of(sec * piece, piece), piece)
    out_ref[:, my_cut] = summed.astype(jnp.bfloat16)

    def z_copy(j):
        spot = out_ref.at[:, my_cut]
        return remote(spot, spot, z_send.at[j - 1], z_recv.at[j - 1], (lax.rem(sec + j, n_sec), ctx))

    for j in range(1, n_sec):
        z_copy(j).start()
    for j in range(1, n_sec):
        z_copy(j).wait_recv()

    @pl.when(core == 0)
    def _():
        to_sibling(0).wait_send()
        to_sibling(1).wait_send()

    for r in range(1, n_chip):

        @pl.when(r > chip)
        def _():
            @pl.when(core == 1)
            def _():
                for c in range(2):
                    chip_copy(r, c, 0).wait_send()
                    chip_copy(r, c, 1).wait_send()

    for j in range(1, n_sec):
        part_copy(j).wait_send()
        z_copy(j).wait_send()


def shared_cache(ret_query, ret_key, ret_value, gate_log, kv_weight):
    n_sec, n_ctx = lax.axis_size("section"), lax.axis_size("ctx")
    n_chip = n_ctx // 2
    rows, width = ret_query.shape
    heads = width // DH
    columns = kv_weight.shape[1]
    piece = columns // n_sec
    gate = jnp.pad(gate_log, ((0, 0), (0, 128 - heads)))
    turned = jnp.pad(gate_log.T, ((0, 8 - heads), (0, 0)))
    state = pltpu.VMEM((heads, DH, DH), jnp.bfloat16)
    total = pltpu.VMEM((8, 128), jnp.float32)
    dma = pltpu.SemaphoreType.DMA
    vmem = pl.BlockSpec(memory_space=pltpu.VMEM)
    return pl.pallas_call(
        functools.partial(cache_kernel, n_sec, n_ctx),
        out_shape=jax.ShapeDtypeStruct((rows, columns), jnp.bfloat16),
        in_specs=[vmem] * 6,
        out_specs=vmem,
        scratch_shapes=[
            pltpu.VMEM((rows, width), jnp.bfloat16),
            pltpu.VMEM((rows, width), jnp.float32),
            state, total, state, total, state, total,
            pltpu.VMEM((n_chip, heads, DH, DH), jnp.bfloat16),
            pltpu.VMEM((n_chip, 8, 128), jnp.float32),
            pltpu.VMEM((heads, DH, DH), jnp.float32),
            pltpu.VMEM((n_sec - 1, rows, piece), jnp.bfloat16),
            pltpu.VMEM((n_sec - 1, rows, piece), jnp.bfloat16),
            dma((2,)), dma((2,)),
            dma((n_chip, 2)), dma((n_chip,)),
            dma((n_chip, 2)), dma((n_chip,)),
            dma((n_sec - 1,)), dma((n_sec - 1,)),
            dma((n_sec - 1,)), dma((n_sec - 1,)),
        ],
        compiler_params=pltpu.CompilerParams(
            collective_id=0, has_side_effects=True, vmem_limit_bytes=LIMIT
        ),
    )(ret_query, ret_key, ret_value, gate, turned, kv_weight)


def attention_kernel(
    n_sec,
    n_ctx,
    q_ref,
    g_ref,
    block_ref,
    att_ref,
    qg_ref,
    out_ref,
    send_sib,
    keep,
    from_sib,
    got_chip,
    kept,
    send_part,
    got_part,
    final,
    gathered,
    cache,
    sib_send,
    sib_recv,
    chip_send,
    chip_recv,
    part_send,
    part_recv,
    all_send,
    all_recv,
    x_send,
    x_recv,
    y_send,
    y_recv,
):
    sec, ctx = lax.axis_index("section"), lax.axis_index("ctx")
    chip, core = lax.div(ctx, 2), lax.rem(ctx, 2)
    n_chip = n_ctx // 2
    sibling = (sec, chip * 2 + 1 - core)
    step = pl.program_id(0)
    kv_heads = kept.shape[0]
    part_heads = kv_heads // n_sec
    layer_count, row_count, width = q_ref.shape
    group = width // DH
    total = n_ctx * row_count
    pair = 2 * row_count
    scale = 1.0 / math.sqrt(DH)

    others = [
        (lax.rem(sec + j, n_sec), chip * 2 + lax.rem(core + c, 2), j, c)
        for j in range(n_sec)
        for c in range(2)
        if j or c
    ]

    my_rows = pl.ds(pl.multiple_of(ctx * row_count, row_count), row_count)

    def rows_of(d):
        return pl.ds(d * row_count, row_count)

    def x_copy(r, h, c):
        spot = cache.at[c, h, my_rows, :]
        return remote(spot, spot, x_send.at[r, h, c], x_recv.at[ctx, h], (sec, 2 * r + c))

    def y_copy(d, h):
        spot = cache.at[core, h, rows_of(d), :]
        return remote(spot, spot, y_send.at[d, h], y_recv.at[d, h], sibling)

    def own_copy(h, c):
        spot = cache.at[c, h, my_rows, :]
        return remote(spot, spot, y_send.at[n_ctx + c, h], y_recv.at[n_ctx + c, h], sibling)

    def hand_out(h):
        for r in range(n_chip - 1, 0, -1):

            @pl.when(r > chip)
            def _():
                for c in range(2):
                    x_copy(r, h, c).start()

        @pl.when(core == 0)
        def _():
            for c in range(2):
                own_copy(h, c).start()

    def forward(h):
        for d in range(n_ctx - 2):

            @pl.when(d < chip * 2)
            def _():
                spot = cache.at[core, h, rows_of(d), :]
                remote(spot, spot, x_send.at[0, h, 0], x_recv.at[d, h], sibling).wait_recv()
                y_copy(d, h).start()

    def arrive(h):
        for d in range(n_ctx - 2):

            @pl.when(d < chip * 2)
            def _():
                spot = cache.at[1 - core, h, rows_of(d), :]
                remote(spot, spot, y_send.at[d, h], y_recv.at[d, h], sibling).wait_recv()

        @pl.when(core == 1)
        def _():
            before = pl.ds(pl.multiple_of(chip * 2 * row_count, row_count), row_count)
            for c in range(2):
                spot = cache.at[c, h, before, :]
                remote(
                    spot, spot, y_send.at[n_ctx + c, h], y_recv.at[n_ctx + c, h], sibling
                ).wait_recv()

    @pl.when(step == 0)
    def _():
        for h in range(kv_heads):
            for c in range(2):
                at = (c * kv_heads + h) * DH
                cache[c, h, my_rows, :] = block_ref[:, at : at + DH]
        greet(
            [(s, d) for s, d, _, _ in others]
            + [
                (sec, lax.rem(chip + i, n_chip) * 2 + c)
                for i in range(1, n_chip)
                for c in range(2)
            ]
        )
        for h in range(min(2, kv_heads)):
            hand_out(h)
        for d in range(1, n_ctx):

            @pl.when(d > ctx)
            def _():
                for c in range(2):
                    for h in range(kv_heads):
                        cache[c, h, d * row_count : (d + 1) * row_count, :] = jnp.zeros(
                            (row_count, DH), jnp.bfloat16
                        )

        forward(0)

    arrive(step)

    def sib_copy(h):
        return remote(send_sib.at[h], from_sib.at[h], sib_send.at[h], sib_recv.at[h], sibling)

    def chip_copy(r, h):
        return remote(
            keep.at[h, r * pair : (r + 1) * pair, :],
            got_chip.at[chip, h],
            chip_send.at[r, h],
            chip_recv.at[chip, h],
            (sec, 2 * r + core),
        )

    def pass_on(h):
        sib_copy(h).wait_recv()
        mine = pl.ds(pl.multiple_of(chip * pair, pair), pair)
        kept[h] = keep[h, mine, :].astype(jnp.float32) + from_sib[h, mine, :].astype(jnp.float32)
        for r in range(n_chip - 1):

            @pl.when(r < chip)
            def _():
                cut = slice(r * pair, (r + 1) * pair)
                keep[h, cut, :] = (
                    keep[h, cut, :].astype(jnp.float32) + from_sib[h, cut, :].astype(jnp.float32)
                ).astype(jnp.bfloat16)
                chip_copy(r, h).start()

    def place_of(h, c):
        return pl.ds(pl.multiple_of((c * kv_heads + h) * DH, DH), DH)

    def part_copy(h):
        owner = lax.div(h, part_heads)
        return remote(
            send_part.at[h],
            got_part.at[sec, h - owner * part_heads],
            part_send.at[h],
            part_recv.at[sec, h - owner * part_heads],
            (owner, ctx),
        )

    def collect(h):
        for r in range(1, n_chip):

            @pl.when(r > chip)
            def _():
                remote(
                    keep.at[h, 0:pair, :],
                    got_chip.at[r, h],
                    chip_send.at[r, h],
                    chip_recv.at[r, h],
                    sibling,
                ).wait_recv()
                kept[h] += got_chip[r, h].astype(jnp.float32)

        @pl.when(sec != lax.div(h, part_heads))
        def _():
            send_part[h] = kept[h].astype(jnp.bfloat16)
            part_copy(h).start()

    def all_copy(h, s, d, j, c):
        index = h - sec * part_heads
        part = pl.ds(pl.multiple_of(lax.rem(core + c, 2) * row_count, row_count), row_count)
        return remote(
            final.at[index, part, :],
            gathered.at[:, place_of(h, core)],
            all_send.at[index, j, c],
            all_recv.at[h, core],
            (s, d),
        )

    def finish(h):
        @pl.when(sec == lax.div(h, part_heads))
        def _():
            index = h - sec * part_heads
            summed = kept[h]
            for j in range(1, n_sec):
                s = lax.rem(sec + j, n_sec)
                remote(
                    send_part.at[h],
                    got_part.at[s, index],
                    part_send.at[h],
                    part_recv.at[s, index],
                    sibling,
                ).wait_recv()
                summed += got_part[s, index].astype(jnp.float32)
            final[index] = summed.astype(jnp.bfloat16)
            for s, d, j, c in others:
                all_copy(h, s, d, j, c).start()
            own = pl.ds(pl.multiple_of(core * row_count, row_count), row_count)
            gathered[:, place_of(h, core)] = final[index, own, :]

    keys = cache[0, step]
    values = cache[1, step]
    keys_turned = keys.T
    values_turned = values.T
    key_place = lax.broadcasted_iota(jnp.int32, (total, row_count), 0)
    row_place = ctx * row_count + lax.broadcasted_iota(jnp.int32, (total, row_count), 1)
    visible = jnp.concatenate([jnp.where(key_place <= row_place, 0.0, -jnp.inf)] * group, axis=1)

    def stacked(ref, layer):
        return jnp.concatenate(
            [ref[layer, :, j * DH : (j + 1) * DH] for j in range(group)], axis=0
        )

    def spread(ref, layer, rows):
        for j in range(group):
            ref[layer, :, j * DH : (j + 1) * DH] = rows[j * row_count : (j + 1) * row_count]

    key_grad = jnp.zeros((total, DH), jnp.float32)
    value_grad = jnp.zeros((total, DH), jnp.float32)
    for layer in range(layer_count):
        queries = stacked(q_ref, layer)
        grads = stacked(g_ref, layer)
        scores = lax.dot_general(
            keys, queries, (((1,), (1,)), ((), ())), preferred_element_type=jnp.float32
        )
        scores = scores * scale + visible
        top = jnp.max(scores, axis=0, keepdims=True)
        soft = jnp.exp(scores - top)
        soft = soft * (1.0 / jnp.sum(soft, axis=0, keepdims=True))
        low = soft.astype(jnp.bfloat16)
        mixed = jnp.dot(values_turned, low, preferred_element_type=jnp.float32)
        mixed = mixed.T.astype(jnp.bfloat16)
        spread(att_ref, layer, mixed)
        product = grads.astype(jnp.float32) * mixed.astype(jnp.float32)
        delta = jnp.sum(product.T, axis=0, keepdims=True)
        prob_grad = lax.dot_general(
            values, grads, (((1,), (1,)), ((), ())), preferred_element_type=jnp.float32
        )
        score_grad = (soft * (prob_grad - delta) * scale).astype(jnp.bfloat16)
        query_grad = jnp.dot(keys_turned, score_grad, preferred_element_type=jnp.float32)
        spread(qg_ref, layer, query_grad.T.astype(jnp.bfloat16))
        key_grad += jnp.dot(score_grad, queries, preferred_element_type=jnp.float32)
        value_grad += jnp.dot(low, grads, preferred_element_type=jnp.float32)
        if layer == 0:

            @pl.when(step < kv_heads - 2)
            def _():
                hand_out(step + 2)

            @pl.when(step < kv_heads - 1)
            def _():
                forward(step + 1)

            @pl.when(step > 0)
            def _():
                pass_on(step - 1)

            @pl.when(step > 1)
            def _():
                collect(step - 2)

            @pl.when(step > 2)
            def _():
                finish(step - 3)

    key_low = key_grad.astype(jnp.bfloat16)
    value_low = value_grad.astype(jnp.bfloat16)

    @pl.when(core == 0)
    def _():
        keep[step] = key_low
        send_sib[step] = value_low

    @pl.when(core == 1)
    def _():
        keep[step] = value_low
        send_sib[step] = key_low

    sib_copy(step).start()

    @pl.when(step == kv_heads - 1)
    def _():
        pass_on(kv_heads - 1)
        for h in range(max(kv_heads - 2, 0), kv_heads):
            collect(h)
        for h in range(max(kv_heads - 3, 0), kv_heads):
            finish(h)
        for h in range(kv_heads):
            for c in range(2):

                @pl.when(jnp.logical_or(sec != h // part_heads, core != c))
                def _():
                    remote(
                        final.at[0, 0:row_count, :],
                        gathered.at[:, place_of(h, c)],
                        all_send.at[0, 0, 0],
                        all_recv.at[h, c],
                        sibling,
                    ).wait_recv()

        out_ref[...] = gathered[...]
        for h in range(kv_heads):
            sib_copy(h).wait_send()
            for r in range(1, n_chip):

                @pl.when(r > chip)
                def _():
                    for c in range(2):
                        x_copy(r, h, c).wait_send()

            for d in range(n_ctx - 2):

                @pl.when(d < chip * 2)
                def _():
                    y_copy(d, h).wait_send()

            @pl.when(core == 0)
            def _():
                for c in range(2):
                    own_copy(h, c).wait_send()

            for r in range(n_chip - 1):

                @pl.when(r < chip)
                def _():
                    chip_copy(r, h).wait_send()

            @pl.when(sec != h // part_heads)
            def _():
                part_copy(h).wait_send()

            @pl.when(sec == h // part_heads)
            def _():
                for s, d, j, c in others:
                    all_copy(h, s, d, j, c).wait_send()


def cross_attention(queries, cotangent, block):
    n_sec, n_ctx = lax.axis_size("section"), lax.axis_size("ctx")
    n_chip = n_ctx // 2
    layer_count, row_count, model_width = queries.shape
    cache_width = block.shape[1]
    total = n_ctx * row_count
    kv_heads = cache_width // 2 // DH
    width = model_width // kv_heads
    pair = 2 * row_count
    part_heads = kv_heads // n_sec
    rows = pl.BlockSpec((layer_count, row_count, width), lambda h: (0, 0, h))
    whole = pl.BlockSpec((row_count, cache_width), lambda h: (0, 0))
    dma = pltpu.SemaphoreType.DMA
    per_head = pltpu.VMEM((kv_heads, total, DH), jnp.bfloat16)
    return pl.pallas_call(
        functools.partial(attention_kernel, n_sec, n_ctx),
        grid=(kv_heads,),
        in_specs=[rows, rows, whole],
        out_specs=[rows, rows, whole],
        out_shape=[
            jax.ShapeDtypeStruct(queries.shape, jnp.bfloat16),
            jax.ShapeDtypeStruct(queries.shape, jnp.bfloat16),
            jax.ShapeDtypeStruct((row_count, cache_width), jnp.bfloat16),
        ],
        scratch_shapes=[
            per_head, per_head, per_head,
            pltpu.VMEM((n_chip, kv_heads, pair, DH), jnp.bfloat16),
            pltpu.VMEM((kv_heads, pair, DH), jnp.float32),
            pltpu.VMEM((kv_heads, pair, DH), jnp.bfloat16),
            pltpu.VMEM((n_sec, part_heads, pair, DH), jnp.bfloat16),
            pltpu.VMEM((part_heads, pair, DH), jnp.bfloat16),
            pltpu.VMEM((row_count, cache_width), jnp.bfloat16),
            pltpu.VMEM((2, kv_heads, total, DH), jnp.bfloat16),
            dma((kv_heads,)), dma((kv_heads,)),
            dma((n_chip, kv_heads)), dma((n_chip, kv_heads)),
            dma((kv_heads,)), dma((n_sec, part_heads)),
            dma((part_heads, n_sec, 2)), dma((kv_heads, 2)),
            dma((n_chip, kv_heads, 2)), dma((n_ctx, kv_heads)),
            dma((n_ctx + 2, kv_heads)), dma((n_ctx + 2, kv_heads)),
        ],
        compiler_params=pltpu.CompilerParams(
            collective_id=1, has_side_effects=True, vmem_limit_bytes=LIMIT
        ),
    )(queries, cotangent, block)


def body(queries, cotangent, ret_query, ret_key, ret_value, gate_log, kv_weight):
    block = shared_cache(ret_query, ret_key, ret_value, gate_log, kv_weight)
    attended_all, grad_rows_all, cache_grad = cross_attention(queries, cotangent, block)
    retention_grad = jnp.einsum(
        "rw,cw->rc", cache_grad, kv_weight, preferred_element_type=jnp.float32
    ).astype(jnp.bfloat16)
    return (attended_all, grad_rows_all, retention_grad)


def solution(mesh):
    return jax.shard_map(
        body,
        mesh=mesh,
        in_specs=(
            P("section", "ctx", None),
            P("section", "ctx", None),
            P("ctx", "section"),
            P("ctx", "section"),
            P("ctx", "section"),
            P("ctx", "section"),
            P("section", None),
        ),
        out_specs=(P("section", "ctx", None), P("section", "ctx", None), P("ctx", "section")),
        check_vma=False,
    )
```
